32 devices in a mesh: ctx: 4 (over y, x), dp: 8 (over z, core).
Axes of the slice: x: 2, y: 2, z: 4, core: 2. Of those that a mesh axis runs over, the one named last changes fastest.
Arguments:
- queries: bfloat16 [8, 4096, 128], P('dp', 'ctx'), may hold values from -24 to 24
- keys: bfloat16 [8, 4096, 128], P('dp', 'ctx'), may hold values from -24 to 24
- values: bfloat16 [8, 4096, 128], P('dp', 'ctx'), may hold values from -6 to 6
- grad_out: bfloat16 [8, 4096, 128], P('dp', 'ctx'), may hold values from -6 to 6
- gain: float32 [1024], P('dp'), may hold values from 0.1 to 1.9
- doc_start: int32 [1, 4096], replicated, may hold values from 0 to 4095, as said below
- win_start: int32 [1, 4096], replicated, may hold values from 0 to 3968, as said below
Outputs:
- grad_queries: bfloat16 [8, 4096, 128], P('dp', 'ctx')
- grad_keys: bfloat16 [8, 4096, 128], P('dp', 'ctx')
- grad_values: bfloat16 [8, 4096, 128], P('dp', 'ctx')
- grad_gain: float32 [1024], P('dp')
The draws below stay inside these ranges and needn't reach their ends.
Inputs may be any that keep to these rules, and one draw needn't show every extreme that they name: Documents are contiguous runs of positions: doc_start of a row is at most its position, equals its own position at a document's first row, and is the same for all rows of a document. win_start is a multiple of 128, at most the start of the row's block of 128 positions and at least (7) * 128 positions before that start.
All inputs are finite; a program needn't handle non-finite values.
Results may differ from the reference program's by a relative error of at most 0.012.
The reference program's roundings to bfloat16 on the way (of `scaled`, `attn_probs` and `score_grad`) count: a program that leaves them out, or rounds other values in their place, can miss the bound.
Values may be sent and summed in bfloat16 or wider, within the bound.
No kernel may reach another device: no remote copies, remote signals or barrier semaphores. Data moves between devices by JAX's collectives and lax.ppermute only.
A program may use at most 64 MiB of HBM per device.

```python
import math
import jax
import jax.numpy as jnp
from jax import lax

HEADS = 8
HD = 128
BLK = 128
WBLK = 8
TOK_DEV = 1024
BH = 8
SEQS = 1
TOKENS = 4096
N_CTX = 4


def paired_fields(key):
    array_shape = (BH, TOKENS, HD)
    query_base = jnp.clip(jax.random.normal(jax.random.fold_in(key, 101), array_shape, jnp.float32), -6.0, 6.0)
    key_base = jnp.clip(jax.random.normal(jax.random.fold_in(key, 102), array_shape, jnp.float32), -6.0, 6.0)
    return (query_base, key_base)


def draw_queries(key, part):
    return paired_fields(key)[0].astype(jnp.bfloat16)


def draw_keys(key, part):
    return paired_fields(key)[1].astype(jnp.bfloat16)


def bounds_pair(key):
    positions = jnp.arange(TOKENS, dtype=jnp.int32)
    start_flags = jax.random.randint(jax.random.fold_in(key, 201), (SEQS, TOKENS), 0, 700) == 0
    start_flags = start_flags | (positions == 0)[None, :] | (positions == TOKENS - 1)[None, :]
    starts = lax.cummax(jnp.where(start_flags, positions[None, :], 0), axis=1).astype(jnp.int32)
    block_index = positions // BLK
    reach_blocks = jax.random.randint(jax.random.fold_in(key, 202), (SEQS, TOKENS // BLK), 0, WBLK).astype(jnp.int32)
    reach_rows = jnp.repeat(reach_blocks, BLK, axis=1)
    window_floor = jnp.maximum(block_index[None, :] - reach_rows, 0) * BLK
    aligned = starts // BLK * BLK
    window = jnp.maximum(aligned, window_floor)
    return (starts, window.astype(jnp.int32))


def draw_doc_start(key, part):
    return bounds_pair(key)[0]


def draw_win_start(key, part):
    return bounds_pair(key)[1]


def steps_of(own_key, dims, shards, smallest, high):
    def one(axis_at, shards_of):
        steps = jax.random.uniform(jax.random.fold_in(jax.random.fold_in(own_key, 6), axis_at), (shards_of,), jnp.float32, smallest / len(shards), high / len(shards))
        return jnp.repeat(jnp.exp(steps), dims[axis_at] // shards_of).reshape((-1,) + (1,) * (len(dims) - axis_at - 1))

    factor_of = one(*shards[0])
    for cut in shards[1:]:
        factor_of = factor_of * one(*cut)
    return factor_of


def bell_draw(rng, dims, width, most, shards=(), kind=jnp.bfloat16):
    entries = width * jax.random.normal(rng, dims, jnp.float32)
    if shards:
        entries = entries * steps_of(rng, dims, shards, -0.22, 0.18)
    return jnp.clip(entries, -most, most).astype(kind)


def setup_inputs(seed: int = 0) -> dict:
    key_of = jax.random.split(jax.random.key(seed), 8)
    return {
        "queries": draw_queries(jax.random.fold_in(key_of[7], 71), 0),
        "keys": draw_keys(jax.random.fold_in(key_of[7], 71), 0),
        "values": bell_draw(key_of[2], (BH, TOKENS, HD), 1.0, 6.0, ((0, 8), (1, 4))),
        "grad_out": bell_draw(key_of[3], (BH, TOKENS, HD), 1.0, 6.0, ((0, 8), (1, 4))),
        "gain": jnp.clip(1.0 + 0.18 * jax.random.normal(key_of[4], (HEADS * HD,), jnp.float32), 0.1, 1.9),
        "doc_start": draw_doc_start(jax.random.fold_in(key_of[7], 71), 0),
        "win_start": draw_win_start(jax.random.fold_in(key_of[7], 71), 0),
    }


def rounded(array):
    return lax.optimization_barrier(array.astype(jnp.bfloat16)).astype(jnp.float32)

def spread(parts, pair_count, tok_rows, head_width):
    summed = jnp.zeros((pair_count, (WBLK - 1) * BLK + tok_rows, head_width), jnp.float32)
    for offset in range(WBLK):
        slab_rows = parts[:, :, offset * BLK:(offset + 1) * BLK].reshape(pair_count, tok_rows, head_width)
        summed = summed + jnp.pad(slab_rows, ((0, 0), (offset * BLK, (WBLK - 1 - offset) * BLK), (0, 0)))
    return summed

def band_grads(scaled, key_ext, value_ext, grad_rows, lower_bound, first_row):
    pair_count, tok_rows, head_width = scaled.shape
    nblock = tok_rows // BLK
    prev_rows = (WBLK - 1) * BLK
    span_cols = WBLK * BLK
    score_scale = 1.0 / math.sqrt(head_width)
    query_blocks = scaled.astype(jnp.float32).reshape(pair_count, nblock, BLK, head_width)
    grad_blocks = grad_rows.astype(jnp.float32).reshape(pair_count, nblock, BLK, head_width)
    key_window = jnp.concatenate([key_ext[:, offset * BLK:offset * BLK + tok_rows].reshape(pair_count, nblock, BLK, head_width) for offset in range(WBLK)], axis=2).astype(jnp.float32)
    value_window = jnp.concatenate([value_ext[:, offset * BLK:offset * BLK + tok_rows].reshape(pair_count, nblock, BLK, head_width) for offset in range(WBLK)], axis=2).astype(jnp.float32)
    query_pos = (first_row + jnp.arange(tok_rows, dtype=jnp.int32)).reshape(nblock, BLK)
    key_pos = first_row - prev_rows + (jnp.arange(nblock, dtype=jnp.int32) * BLK)[:, None] + jnp.arange(span_cols, dtype=jnp.int32)[None, :]
    visible = (key_pos[:, None, :] >= lower_bound.reshape(nblock, BLK)[:, :, None]) & (key_pos[:, None, :] <= query_pos[:, :, None])
    scores = jnp.einsum('bnqd,bnkd->bnqk', query_blocks, key_window) * score_scale
    scores = jnp.where(visible[None], scores, -jnp.inf)
    weights = jnp.exp(scores - lax.optimization_barrier(jnp.max(scores, axis=-1, keepdims=True)))
    attn_probs = rounded(weights / lax.optimization_barrier(jnp.sum(weights, axis=-1, keepdims=True)))
    prob_grad = jnp.einsum('bnqd,bnkd->bnqk', grad_blocks, value_window)
    row_delta = lax.optimization_barrier(jnp.sum(attn_probs * prob_grad, axis=-1, keepdims=True))
    score_grad = rounded(attn_probs * (prob_grad - row_delta))
    grad_scaled = jnp.einsum('bnqk,bnkd->bnqd', score_grad, key_window) * score_scale
    key_parts = jnp.einsum('bnqk,bnqd->bnkd', score_grad, query_blocks) * score_scale
    value_parts = jnp.einsum('bnqk,bnqd->bnkd', attn_probs, grad_blocks)
    return (grad_scaled.reshape(pair_count, tok_rows, head_width), spread(key_parts, pair_count, tok_rows, head_width), spread(value_parts, pair_count, tok_rows, head_width))

def to_heads(array):
    return array.reshape(SEQS, HEADS, TOKENS, HD)

def reference(queries, keys, values, grad_out, gain, doc_start, win_start):
    prev_rows = (WBLK - 1) * BLK
    gain_rows = gain.reshape(HEADS, HD)

    def one_sequence(inputs):
        seq_query, seq_key, seq_value, seq_grad, seq_doc, seq_win = inputs
        scaled = lax.optimization_barrier((seq_query.astype(jnp.float32) * gain_rows[:, None, :]).astype(jnp.bfloat16))
        lower_bound = jnp.maximum(seq_doc, seq_win)
        pad_zeros = jnp.zeros((HEADS, prev_rows, HD), seq_key.dtype)
        padded_key = jnp.concatenate([pad_zeros, seq_key], axis=1)
        padded_value = jnp.concatenate([pad_zeros, seq_value], axis=1)
        key_total = jnp.zeros((HEADS, prev_rows + TOKENS, HD), jnp.float32)
        value_total = jnp.zeros((HEADS, prev_rows + TOKENS, HD), jnp.float32)
        grad_pieces = []
        for shard_index in range(N_CTX):
            first_row = shard_index * TOK_DEV
            last_row = first_row + TOK_DEV
            grad_scaled, key_grad, value_grad = band_grads(scaled[:, first_row:last_row], padded_key[:, first_row:first_row + prev_rows + TOK_DEV], padded_value[:, first_row:first_row + prev_rows + TOK_DEV], seq_grad[:, first_row:last_row], lower_bound[first_row:last_row], first_row)
            key_total = key_total.at[:, first_row + prev_rows:last_row + prev_rows].add(key_grad[:, prev_rows:])
            key_total = key_total.at[:, first_row:first_row + prev_rows].add(rounded(key_grad[:, :prev_rows]))
            value_total = value_total.at[:, first_row + prev_rows:last_row + prev_rows].add(value_grad[:, prev_rows:])
            value_total = value_total.at[:, first_row:first_row + prev_rows].add(rounded(value_grad[:, :prev_rows]))
            grad_pieces.append(grad_scaled)
        grad_all = jnp.concatenate(grad_pieces, axis=1)
        grad_query = (grad_all * gain_rows[:, None, :]).astype(jnp.bfloat16)
        grad_heads = lax.optimization_barrier(jnp.sum(grad_all * seq_query.astype(jnp.float32), axis=1))
        return (grad_query, key_total[:, prev_rows:].astype(jnp.bfloat16), value_total[:, prev_rows:].astype(jnp.bfloat16), grad_heads)
    grad_query, grad_key, grad_value, grad_heads = lax.map(one_sequence, (to_heads(queries), to_heads(keys), to_heads(values), to_heads(grad_out), doc_start, win_start))
    return (grad_query.reshape(BH, TOKENS, HD), grad_key.reshape(BH, TOKENS, HD), grad_value.reshape(BH, TOKENS, HD), lax.optimization_barrier(jnp.sum(grad_heads, axis=0)).reshape(HEADS * HD))
```

```python
import functools
import math

import jax
import jax.numpy as jnp
from jax import lax
from jax.experimental import pallas as pl
from jax.experimental.pallas import tpu as pltpu
from jax.sharding import PartitionSpec as P

HEADS = 8
BLK = 128
WBLK = 8
PREV = (WBLK - 1) * BLK
GROUP = 2 * BLK
LOG2E = 1.4426950408889634
NEG = -1e30
M_ROW, L_ROW, D_ROW = 0, 1, 2


def shift(value, axis, by):
    length = lax.axis_size(axis)
    pairs = [(i, (i + by) % length) for i in range(length)]
    return lax.ppermute(value, axis, pairs)


def mm(left, right):
    return lax.dot_general(left, right, (((1,), (0,)), ((), ())), preferred_element_type=jnp.float32)


def mm_t(left, right):
    return lax.dot_general(left, right, (((1,), (1,)), ((), ())), preferred_element_type=jnp.float32)


def scaled_rows(q_ref, gain_ref, start, width):
    rows = q_ref[0, start : start + width, :].astype(jnp.float32) * gain_ref[0]
    return rows.astype(jnp.bfloat16)


def own_logits(k_ref, scaled, low_ref, start, width, factor):
    stop = start + width
    logits = mm_t(k_ref[0, :stop, :], scaled) * factor
    key_at = lax.broadcasted_iota(jnp.int32, (stop, width), 0)
    query_at = start + lax.broadcasted_iota(jnp.int32, (stop, width), 1)
    visible = (key_at >= low_ref[:, start:stop]) & (key_at <= query_at)
    return jnp.where(visible, logits, NEG)


def stats_kernel(q_ref, k_ref, v_ref, g_ref, gain_ref, low_ref, stats_ref, *, factor):
    rows = q_ref.shape[1]
    for start in range(0, rows, GROUP):
        width = min(GROUP, rows - start)
        stop = start + width
        scaled = scaled_rows(q_ref, gain_ref, start, width)
        logits = own_logits(k_ref, scaled, low_ref, start, width, factor)
        top = jnp.max(logits, axis=0, keepdims=True)
        weights = jnp.exp2(logits - top)
        prob_grad = mm_t(v_ref[0, :stop, :], g_ref[0, start:stop, :])
        stats_ref[0, M_ROW : M_ROW + 1, start:stop] = top
        stats_ref[0, L_ROW : L_ROW + 1, start:stop] = jnp.sum(weights, axis=0, keepdims=True)
        stats_ref[0, D_ROW : D_ROW + 1, start:stop] = jnp.sum(weights * prob_grad, axis=0, keepdims=True)


def halo_kernel(
    q_ref, g_ref, gain_ref, low_ref, part_ref, kv_ref,
    stats_ref, dq_ref, dkv_ref, probs_ref, grads_ref, *, factor, score_scale,
):
    rows = q_ref.shape[1]
    key_cols = kv_ref[0, 0].T
    for start in range(0, PREV, GROUP):
        width = min(GROUP, PREV - start)
        stop = start + width
        scaled = scaled_rows(q_ref, gain_ref, start, width)
        logits = mm_t(kv_ref[0, 0, start:, :], scaled) * factor
        key_at = (start - PREV) + lax.broadcasted_iota(jnp.int32, (PREV - start, width), 0)
        logits = jnp.where(key_at >= low_ref[:, start:stop], logits, NEG)
        own_top = part_ref[0, M_ROW : M_ROW + 1, start:stop]
        top = jnp.maximum(own_top, jnp.max(logits, axis=0, keepdims=True))
        weights = jnp.exp2(logits - top)
        prob_grad = mm_t(kv_ref[1, 0, start:, :], g_ref[0, start:stop, :])
        shrink = jnp.exp2(own_top - top)
        total = part_ref[0, L_ROW : L_ROW + 1, start:stop] * shrink + jnp.sum(weights, axis=0, keepdims=True)
        inverse = 1.0 / total
        delta = (
            part_ref[0, D_ROW : D_ROW + 1, start:stop] * shrink
            + jnp.sum(weights * prob_grad, axis=0, keepdims=True)
        ) * inverse
        stats_ref[0, M_ROW : M_ROW + 1, start:stop] = top
        stats_ref[0, L_ROW : L_ROW + 1, start:stop] = inverse
        stats_ref[0, D_ROW : D_ROW + 1, start:stop] = delta
        probs = (weights * inverse).astype(jnp.bfloat16)
        grads = (probs.astype(jnp.float32) * (prob_grad - delta)).astype(jnp.bfloat16)
        probs_ref[start:, start:stop] = probs
        grads_ref[start:, start:stop] = grads
        dq_ref[0, start:stop, :] = mm(key_cols[:, start:], grads).T
    for start in range(PREV, rows, BLK):
        stop = start + BLK
        inverse = 1.0 / part_ref[0, L_ROW : L_ROW + 1, start:stop]
        stats_ref[0, M_ROW : M_ROW + 1, start:stop] = part_ref[0, M_ROW : M_ROW + 1, start:stop]
        stats_ref[0, L_ROW : L_ROW + 1, start:stop] = inverse
        stats_ref[0, D_ROW : D_ROW + 1, start:stop] = part_ref[0, D_ROW : D_ROW + 1, start:stop] * inverse
    for first in range(0, PREV, GROUP):
        last = min(first + GROUP, PREV)
        all_scaled = scaled_rows(q_ref, gain_ref, 0, last)
        dkv_ref[0, 0, first:last, :] = (mm(grads_ref[first:last, :last], all_scaled) * score_scale).astype(
            jnp.bfloat16
        )
        dkv_ref[1, 0, first:last, :] = mm(probs_ref[first:last, :last], g_ref[0, :last, :]).astype(jnp.bfloat16)


def own_kernel(
    q_ref, k_ref, v_ref, g_ref, gain_ref, low_ref, stats_ref, dqh_ref,
    gq_ref, dk_ref, dv_ref, head_ref, probs_ref, grads_ref, *, factor, score_scale,
):
    rows = q_ref.shape[1]
    key_cols = k_ref[0].T
    head_sum = jnp.zeros((1, q_ref.shape[2]), jnp.float32)
    for start in range(0, rows, GROUP):
        width = min(GROUP, rows - start)
        stop = start + width
        scaled = scaled_rows(q_ref, gain_ref, start, width)
        logits = own_logits(k_ref, scaled, low_ref, start, width, factor)
        weights = jnp.exp2(logits - stats_ref[0, M_ROW : M_ROW + 1, start:stop])
        prob_grad = mm_t(v_ref[0, :stop, :], g_ref[0, start:stop, :])
        probs = (weights * stats_ref[0, L_ROW : L_ROW + 1, start:stop]).astype(jnp.bfloat16)
        delta = stats_ref[0, D_ROW : D_ROW + 1, start:stop]
        grads = (probs.astype(jnp.float32) * (prob_grad - delta)).astype(jnp.bfloat16)
        probs_ref[:stop, start:stop] = probs
        grads_ref[:stop, start:stop] = grads
        dq = mm(key_cols[:, :stop], grads).T
        halo = min(stop, PREV) - start
        if halo < width:
            zeros = jnp.zeros((width - max(halo, 0), dq.shape[1]), jnp.float32)
            extra = jnp.concatenate([dqh_ref[0, start : start + halo, :], zeros], axis=0) if halo > 0 else zeros
        else:
            extra = dqh_ref[0, start:stop, :]
        dq = (dq + extra) * score_scale
        gq_ref[0, start:stop, :] = (dq * gain_ref[0]).astype(jnp.bfloat16)
        head_sum = head_sum + jnp.sum(
            dq * q_ref[0, start:stop, :].astype(jnp.float32), axis=0, keepdims=True
        )
    head_ref[0] = head_sum
    for first in range(0, rows, GROUP):
        last = min(first + GROUP, rows)
        late_scaled = scaled_rows(q_ref, gain_ref, first, rows - first)
        dk_ref[0, first:last, :] = mm(grads_ref[first:last, first:], late_scaled) * score_scale
        dv_ref[0, first:last, :] = mm(probs_ref[first:last, first:], g_ref[0, first:, :])


def whole(shape):
    return pl.BlockSpec((1,) + shape, lambda p: (p,) + (0,) * len(shape))


def ctx_sum(value, axis):
    length = lax.axis_size(axis)
    if length > 4:
        return lax.psum(value, axis)
    total = value
    for by in range(1, length):
        total = total + shift(value, axis, by)
    return total


def on_device(queries, keys, values, grad_out, gain, doc_start, win_start):
    pair_count, rows, width = queries.shape
    score_scale = 1.0 / math.sqrt(width)
    factor = score_scale * LOG2E
    first_row = lax.axis_index("ctx") * rows
    first_pair = lax.axis_index("dp") * pair_count
    head_first = first_pair % HEADS
    seq_index = first_pair // HEADS
    aligned = lax.axis_size("dp") * pair_count == HEADS and gain.shape[0] == pair_count * width

    tail = jnp.stack([keys[:, rows - PREV :], values[:, rows - PREV :]])
    halo = shift(tail, "ctx", 1)

    if aligned:
        gain_rows = gain.reshape(pair_count, 1, width)
    else:
        full_gain = lax.all_gather(gain, "dp", axis=0, tiled=True)
        gain_rows = lax.dynamic_slice_in_dim(
            full_gain.reshape(HEADS, width), head_first, pair_count, 0
        ).reshape(pair_count, 1, width)
    lower = jnp.maximum(
        lax.dynamic_slice(doc_start, (seq_index, first_row), (1, rows)),
        lax.dynamic_slice(win_start, (seq_index, first_row), (1, rows)),
    )
    block_floor = (jnp.arange(rows, dtype=jnp.int32) // BLK - (WBLK - 1)) * BLK
    lower = jnp.maximum(lower - first_row, block_floor[None, :])

    row_spec = whole((rows, width))
    gain_spec = whole((1, width))
    stat_spec = whole((8, rows))
    prev_spec = whole((PREV, width))
    low_spec = pl.BlockSpec((1, rows), lambda p: (0, 0))
    kv_spec = pl.BlockSpec((2, 1, PREV, width), lambda p: (0, p, 0, 0))
    params = pltpu.CompilerParams(vmem_limit_bytes=48 * 1024 * 1024)
    stat_shape = jax.ShapeDtypeStruct((pair_count, 8, rows), jnp.float32)

    part = pl.pallas_call(
        functools.partial(stats_kernel, factor=factor),
        grid=(pair_count,),
        in_specs=[row_spec] * 4 + [gain_spec, low_spec],
        out_specs=stat_spec,
        out_shape=stat_shape,
        compiler_params=params,
        cost_estimate=pl.CostEstimate(flops=4 * rows * rows * width, bytes_accessed=8 * rows * width, transcendentals=rows * rows),
    )(queries, keys, values, grad_out, gain_rows, lower)

    stats, dq_halo, dkv_halo = pl.pallas_call(
        functools.partial(halo_kernel, factor=factor, score_scale=score_scale),
        grid=(pair_count,),
        in_specs=[row_spec] * 2 + [gain_spec, low_spec, stat_spec, kv_spec],
        out_specs=(stat_spec, prev_spec, kv_spec),
        out_shape=(
            stat_shape,
            jax.ShapeDtypeStruct((pair_count, PREV, width), jnp.float32),
            jax.ShapeDtypeStruct((2, pair_count, PREV, width), jnp.bfloat16),
        ),
        scratch_shapes=[pltpu.VMEM((PREV, PREV), jnp.bfloat16)] * 2,
        compiler_params=params,
        cost_estimate=pl.CostEstimate(flops=6 * rows * rows * width, bytes_accessed=8 * rows * width, transcendentals=rows * rows),
    )(queries, grad_out, gain_rows, lower, part, halo)

    returned = shift(dkv_halo, "ctx", -1)

    grad_queries, dk_own, dv_own, head_terms = pl.pallas_call(
        functools.partial(own_kernel, factor=factor, score_scale=score_scale),
        grid=(pair_count,),
        in_specs=[row_spec] * 4 + [gain_spec, low_spec, stat_spec, prev_spec],
        out_specs=(row_spec, row_spec, row_spec, gain_spec),
        out_shape=(
            jax.ShapeDtypeStruct((pair_count, rows, width), jnp.bfloat16),
            jax.ShapeDtypeStruct((pair_count, rows, width), jnp.float32),
            jax.ShapeDtypeStruct((pair_count, rows, width), jnp.float32),
            jax.ShapeDtypeStruct((pair_count, 1, width), jnp.float32),
        ),
        scratch_shapes=[pltpu.VMEM((rows, rows), jnp.bfloat16)] * 2,
        compiler_params=params,
        cost_estimate=pl.CostEstimate(flops=10 * rows * rows * width, bytes_accessed=16 * rows * width, transcendentals=rows * rows),
    )(queries, keys, values, grad_out, gain_rows, lower, stats, dq_halo)

    if aligned:
        grad_gain = ctx_sum(head_terms, "ctx").reshape(pair_count * width)
    else:
        gain_table = lax.dynamic_update_slice_in_dim(
            jnp.zeros((HEADS, width), jnp.float32), head_terms.reshape(pair_count, width), head_first, 0
        ).reshape(HEADS * width)
        everything = lax.psum(gain_table, ("ctx", "dp"))
        share = gain.shape[0]
        grad_gain = lax.dynamic_slice_in_dim(everything, lax.axis_index("dp") * share, share, 0)

    def joined(own, back):
        return own.at[:, rows - PREV :].add(back.astype(jnp.float32)).astype(jnp.bfloat16)

    return (grad_queries, joined(dk_own, returned[0]), joined(dv_own, returned[1]), grad_gain)


def solution(mesh):
    rows = P("dp", "ctx", None)
    return jax.shard_map(
        on_device,
        mesh=mesh,
        in_specs=(rows, rows, rows, rows, P("dp"), P(), P()),
        out_specs=(rows, rows, rows, P("dp")),
        check_vma=False,
    )
```

```python
import functools
import math

import jax
import jax.numpy as jnp
from jax import lax
from jax.experimental import pallas as pl
from jax.experimental.pallas import tpu as pltpu
from jax.sharding import PartitionSpec as P

HEADS = 8
BLK = 128
WBLK = 8
PREV = (WBLK - 1) * BLK
GROUP = 2 * BLK
LOG2E = 1.4426950408889634
NEG = -1e30
M_ROW, L_ROW, D_ROW = 0, 1, 2
LIGHT, HEAVY = 1, 10**10


def shift(value, axis, by):
    length = lax.axis_size(axis)
    pairs = [(i, (i + by) % length) for i in range(length)]
    return lax.ppermute(value, axis, pairs)


def mm(left, right):
    return lax.dot_general(left, right, (((1,), (0,)), ((), ())), preferred_element_type=jnp.float32)


def mm_t(left, right):
    return lax.dot_general(left, right, (((1,), (1,)), ((), ())), preferred_element_type=jnp.float32)


def groups(rows):
    return [(start, min(start + GROUP, rows)) for start in range(0, rows, GROUP)]


def halo_chunks(halo, rows):
    ahead = PREV - halo
    return [
        (max(0, start - ahead), min(halo, stop - ahead), min(stop, PREV))
        for start, stop in groups(rows)
        if start < PREV and stop > ahead
    ]


def halo_from(start, halo):
    return max(0, start - (PREV - halo))


def own_stats_kernel(
    q_hbm, k_hbm, v_hbm, g_hbm, gain_ref, low_ref,
    q_ref, g_ref, scaled_ref, keyt_ref, stats_ref, weight_ref, slope_ref, k_ref, v_ref, sems, *, factor,
):
    pair = pl.program_id(0)
    copies = [
        pltpu.make_async_copy(source.at[pair], target, sems.at[i])
        for i, (source, target) in enumerate(
            ((q_hbm, q_ref.at[0]), (k_hbm, k_ref), (v_hbm, v_ref), (g_hbm, g_ref.at[0]))
        )
    ]
    for copy in copies:
        copy.start()
    for copy in copies:
        copy.wait()
    rows = q_ref.shape[1]
    keyt_ref[0] = k_ref[...].T
    scaled_ref[0] = (q_ref[0].astype(jnp.float32) * gain_ref[0]).astype(jnp.bfloat16)
    for start, stop in groups(rows):
        logits = mm_t(k_ref[:stop, :], scaled_ref[0, start:stop, :]) * factor
        key_at = lax.broadcasted_iota(jnp.int32, logits.shape, 0)
        query_at = start + lax.broadcasted_iota(jnp.int32, logits.shape, 1)
        visible = (key_at >= low_ref[:, start:stop]) & (key_at <= query_at)
        logits = jnp.where(visible, logits, NEG)
        top = jnp.max(logits, axis=0, keepdims=True)
        weights = jnp.exp2(logits - top)
        slopes = mm_t(v_ref[:stop, :], g_ref[0, start:stop, :])
        weight_ref[0, :stop, start:stop] = weights
        slope_ref[0, :stop, start:stop] = slopes
        stats_ref[0, M_ROW : M_ROW + 1, start:stop] = top
        stats_ref[0, L_ROW : L_ROW + 1, start:stop] = jnp.sum(weights, axis=0, keepdims=True)
        stats_ref[0, D_ROW : D_ROW + 1, start:stop] = jnp.sum(weights * slopes, axis=0, keepdims=True)


def probs_kernel(
    scaled_ref, g_ref, low_ref, part_ref, weight_ref, kh_ref,
    delta_ref, hprobs_ref, probs_ref, dv_ref, *, factor,
):
    rows = scaled_ref.shape[1]
    halo = kh_ref.shape[1]
    for start, stop in groups(rows):
        own_top = part_ref[0, M_ROW : M_ROW + 1, start:stop]
        total = part_ref[0, L_ROW : L_ROW + 1, start:stop]
        if start < PREV:
            first = halo_from(start, halo)
            logits = mm_t(kh_ref[0, first:, :], scaled_ref[0, start:stop, :]) * factor
            key_at = (first - halo) + lax.broadcasted_iota(jnp.int32, logits.shape, 0)
            logits = jnp.where(key_at >= low_ref[:, start:stop], logits, NEG)
            top = jnp.maximum(own_top, jnp.max(logits, axis=0, keepdims=True))
            weights = jnp.exp2(logits - top)
            shrink = jnp.exp2(own_top - top)
            total = total * shrink + jnp.sum(weights, axis=0, keepdims=True)
            inverse = 1.0 / total
            hprobs_ref[0, first:, start:stop] = (weights * inverse).astype(jnp.bfloat16)
            share = shrink * inverse
        else:
            share = 1.0 / total
        delta_ref[0, 0:1, start:stop] = part_ref[0, D_ROW : D_ROW + 1, start:stop] * share
        probs_ref[0, :stop, start:stop] = (weight_ref[0, :stop, start:stop] * share).astype(jnp.bfloat16)
    for first, last, seen in halo_chunks(halo, rows):
        dv_ref[0, first:last, :] = mm(hprobs_ref[0, first:last, :seen], g_ref[0, :seen, :]).astype(jnp.bfloat16)


def grads_kernel(
    q_ref, scaled_ref, g_ref, keyt_ref, part_ref, hprobs_ref, probs_ref, slope_ref, kh_ref, vh_ref,
    dq_ref, dk_ref, head_ref, grads_ref, hgrads_ref, *, score_scale,
):
    rows = q_ref.shape[1]
    halo = kh_ref.shape[1]
    halo_cols = kh_ref[0].T
    head_sum = jnp.zeros((1, q_ref.shape[2]), jnp.float32)
    for start, stop in groups(rows):
        delta = part_ref[0, 0:1, start:stop]
        if start < PREV:
            first = halo_from(start, halo)
            probs = hprobs_ref[0, first:, start:stop].astype(jnp.float32)
            slopes = mm_t(vh_ref[0, first:, :], g_ref[0, start:stop, :])
            delta = delta + jnp.sum(probs * slopes, axis=0, keepdims=True)
            hgrads = (probs * (slopes - delta)).astype(jnp.bfloat16)
            hgrads_ref[first:, start:stop] = hgrads
        probs = probs_ref[0, :stop, start:stop].astype(jnp.float32)
        grads = (probs * (slope_ref[0, :stop, start:stop] - delta)).astype(jnp.bfloat16)
        grads_ref[0, :stop, start:stop] = grads
        dq = mm(keyt_ref[0, :, :stop], grads)
        if start < PREV:
            dq = dq + mm(halo_cols[:, first:], hgrads)
        dq = dq.T * score_scale
        dq_ref[0, start:stop, :] = dq
        head_sum = head_sum + jnp.sum(dq * q_ref[0, start:stop, :].astype(jnp.float32), axis=0, keepdims=True)
    head_ref[0] = head_sum
    for first, last, seen in halo_chunks(halo, rows):
        dk_ref[0, first:last, :] = (mm(hgrads_ref[first:last, :seen], scaled_ref[0, :seen, :]) * score_scale).astype(
            jnp.bfloat16
        )


def own_keys_kernel(
    g_ref, scaled_ref, probs_ref, grads_ref, dq_ref, gain_ref, back_ref, gq_ref, dv_ref, dk_ref, *, score_scale
):
    rows = g_ref.shape[1]
    gq_ref[0] = (dq_ref[0] * gain_ref[0]).astype(jnp.bfloat16)
    lead = rows - back_ref.shape[1]
    for first, last in groups(rows):
        own = mm(probs_ref[0, first:last, first:], g_ref[0, first:, :])
        cut = min(max(lead - first, 0), last - first)
        if cut:
            dv_ref[0, first : first + cut, :] = own[:cut].astype(jnp.bfloat16)
        if cut < last - first:
            back = back_ref[0, first + cut - lead : last - lead, :].astype(jnp.float32)
            dv_ref[0, first + cut : last, :] = (own[cut:] + back).astype(jnp.bfloat16)
        dk_ref[0, first:last, :] = mm(grads_ref[0, first:last, first:], scaled_ref[0, first:, :]) * score_scale


def finish_kernel(own_ref, back_ref, *refs):
    terms, (dk_ref, gain_ref) = refs[:-2], refs[-2:]
    lead = own_ref.shape[1] - back_ref.shape[1]
    if lead:
        dk_ref[0, :lead, :] = own_ref[0, :lead, :].astype(jnp.bfloat16)
    dk_ref[0, lead:, :] = (own_ref[0, lead:, :] + back_ref[0].astype(jnp.float32)).astype(jnp.bfloat16)
    total = terms[0][...]
    for term in terms[1:]:
        total = total + term[...]
    gain_ref[...] = total


def whole(shape):
    return pl.BlockSpec((1,) + shape, lambda p: (p,) + (0,) * len(shape))


def band(halo, queries, keys, values, grad_out, gain_rows, lower, aligned):
    pair_count, rows, width = queries.shape
    score_scale = 1.0 / math.sqrt(width)
    factor = score_scale * LOG2E
    bf16, f32 = jnp.bfloat16, jnp.float32
    key_halo = shift(keys[:, rows - halo :], "ctx", 1)
    value_halo = shift(values[:, rows - halo :], "ctx", 1)

    row_spec = whole((rows, width))
    gain_spec = whole((1, width))
    stat_spec = whole((8, rows))
    delta_spec = whole((1, rows))
    halo_spec = whole((halo, width))
    keyt_spec = whole((width, rows))
    own_sq = whole((rows, rows))
    halo_sq = whole((halo, rows))
    low_spec = pl.BlockSpec((1, rows), lambda p: (0, 0))
    hbm = pl.BlockSpec(memory_space=pltpu.HBM)

    def shaped(shape, dtype):
        return jax.ShapeDtypeStruct((pair_count,) + shape, dtype)

    def call(kernel, in_specs, outs, weight, scratch=(), **fixed):
        specs, shapes = zip(*outs)
        return pl.pallas_call(
            functools.partial(kernel, **fixed),
            grid=(pair_count,),
            in_specs=in_specs,
            out_specs=specs,
            out_shape=shapes,
            scratch_shapes=list(scratch),
            compiler_params=pltpu.CompilerParams(vmem_limit_bytes=32 * 1024 * 1024),
            cost_estimate=pl.CostEstimate(flops=weight, bytes_accessed=1, transcendentals=0),
        )

    row_out = (row_spec, shaped((rows, width), bf16))
    wide_out = (row_spec, shaped((rows, width), f32))
    halo_out = (halo_spec, shaped((halo, width), bf16))
    queries_in, grad_in, scaled, key_cols, part, own_weights, own_slopes = call(
        own_stats_kernel,
        [hbm] * 4 + [gain_spec, low_spec],
        (
            row_out,
            row_out,
            row_out,
            (keyt_spec, shaped((width, rows), bf16)),
            (stat_spec, shaped((8, rows), f32)),
            (own_sq, shaped((rows, rows), f32)),
            (own_sq, shaped((rows, rows), f32)),
        ),
        LIGHT,
        scratch=[pltpu.VMEM((rows, width), bf16)] * 2 + [pltpu.SemaphoreType.DMA((4,))],
        factor=factor,
    )(*(pltpu.with_memory_space_constraint(x, pltpu.HBM) for x in (queries, keys, values, grad_out)), gain_rows, lower)

    own_delta, halo_probs, own_probs, dv_halo = call(
        probs_kernel,
        [row_spec, row_spec, low_spec, stat_spec, own_sq, halo_spec],
        (
            (delta_spec, shaped((1, rows), f32)),
            (halo_sq, shaped((halo, rows), bf16)),
            (own_sq, shaped((rows, rows), bf16)),
            halo_out,
        ),
        LIGHT,
        factor=factor,
    )(scaled, grad_in, lower, part, own_weights, key_halo)
    dv_back = shift(dv_halo, "ctx", -1)

    dq, dk_halo, head_terms, own_grads = call(
        grads_kernel,
        [row_spec] * 3 + [keyt_spec, delta_spec, halo_sq, own_sq, own_sq, halo_spec, halo_spec],
        (
            wide_out,
            halo_out,
            (gain_spec, shaped((1, width), f32)),
            (own_sq, shaped((rows, rows), bf16)),
        ),
        HEAVY,
        scratch=[pltpu.VMEM((halo, rows), bf16)],
        score_scale=score_scale,
    )(
        queries_in, scaled, grad_in, key_cols, own_delta, halo_probs, own_probs, own_slopes,
        key_halo, value_halo,
    )
    dk_back = shift(dk_halo, "ctx", -1)
    terms = [head_terms]
    if aligned:
        length = lax.axis_size("ctx")
        if length <= 4:
            terms += [shift(head_terms, "ctx", by) for by in range(1, length)]
        else:
            terms = [lax.psum(head_terms, "ctx")]

    grad_queries, grad_values, dk_own = call(
        own_keys_kernel,
        [row_spec, row_spec, own_sq, own_sq, row_spec, gain_spec, halo_spec],
        (row_out, row_out, wide_out),
        LIGHT,
        score_scale=score_scale,
    )(grad_in, scaled, own_probs, own_grads, dq, gain_rows, dv_back)
    grad_keys, gain_sum = call(
        finish_kernel,
        [row_spec, halo_spec] + [gain_spec] * len(terms),
        (row_out, (gain_spec, shaped((1, width), f32))),
        LIGHT,
    )(dk_own, dk_back, *terms)
    return grad_queries, grad_keys, grad_values, gain_sum


def on_device(queries, keys, values, grad_out, gain, doc_start, win_start):
    pair_count, rows, width = queries.shape
    first_row = lax.axis_index("ctx") * rows
    first_pair = lax.axis_index("dp") * pair_count
    head_first = first_pair % HEADS
    seq_index = first_pair // HEADS
    aligned = lax.axis_size("dp") * pair_count == HEADS and gain.shape[0] == pair_count * width
    if aligned:
        gain_rows = gain.reshape(pair_count, 1, width)
    else:
        full_gain = lax.all_gather(gain, "dp", axis=0, tiled=True)
        gain_rows = lax.dynamic_slice_in_dim(
            full_gain.reshape(HEADS, width), head_first, pair_count, 0
        ).reshape(pair_count, 1, width)
    lower = jnp.maximum(
        lax.dynamic_slice(doc_start, (seq_index, first_row), (1, rows)),
        lax.dynamic_slice(win_start, (seq_index, first_row), (1, rows)),
    )
    block_floor = (jnp.arange(rows, dtype=jnp.int32) // BLK - (WBLK - 1)) * BLK
    lower = jnp.maximum(lower - first_row, block_floor[None, :])

    grad_queries, grad_keys, grad_values, gain_sum = band(
        PREV, queries, keys, values, grad_out, gain_rows, lower, aligned
    )
    if aligned:
        grad_gain = gain_sum.reshape(pair_count * width)
    else:
        gain_table = lax.dynamic_update_slice_in_dim(
            jnp.zeros((HEADS, width), jnp.float32), gain_sum.reshape(pair_count, width), head_first, 0
        ).reshape(HEADS * width)
        everything = lax.psum(gain_table, ("ctx", "dp"))
        share = gain.shape[0]
        grad_gain = lax.dynamic_slice_in_dim(everything, lax.axis_index("dp") * share, share, 0)
    return (grad_queries, grad_keys, grad_values, grad_gain)


def solution(mesh):
    rows = P("dp", "ctx", None)
    return jax.shard_map(
        on_device,
        mesh=mesh,
        in_specs=(rows, rows, rows, rows, P("dp"), P(), P()),
        out_specs=(rows, rows, rows, P("dp")),
        check_vma=False,
    )
```

```python
import functools
import math

import jax
import jax.numpy as jnp
from jax import lax
from jax.experimental import pallas as pl
from jax.experimental.pallas import tpu as pltpu
from jax.sharding import PartitionSpec as P

HEADS = 8
BLK = 128
WBLK = 8
PREV = (WBLK - 1) * BLK
GROUP = 2 * BLK
LOG2E = 1.4426950408889634
NEG = -1e30
M_ROW, L_ROW, D_ROW = 0, 1, 2
LIGHT, HEAVY = 1, 10**10
FEWEST = 3
RIDERS = 16


def shift(value, axis, by):
    length = lax.axis_size(axis)
    pairs = [(i, (i + by) % length) for i in range(length)]
    return lax.ppermute(value, axis, pairs)


def mm(left, right):
    return lax.dot_general(left, right, (((1,), (0,)), ((), ())), preferred_element_type=jnp.float32)


def mm_t(left, right):
    return lax.dot_general(left, right, (((1,), (1,)), ((), ())), preferred_element_type=jnp.float32)


def groups(rows):
    return [(start, min(start + GROUP, rows)) for start in range(0, rows, GROUP)]


def halo_chunks(halo, rows):
    ahead = PREV - halo
    return [
        (max(0, start - ahead), min(halo, stop - ahead), min(stop, PREV))
        for start, stop in groups(rows)
        if start < PREV and stop > ahead
    ]


def halo_from(start, halo):
    return max(0, start - (PREV - halo))


def load_kernel(
    doc_hbm, win_hbm, k_hbm, v_hbm, q_hbm, g_hbm,
    k_ref, v_ref, q_ref, g_ref, low_ref, size_ref, doc_ref, win_ref, sems,
):
    pair = pl.program_id(0)
    moves = [(doc_hbm, doc_ref), (win_hbm, win_ref)]
    moves += [
        (source.at[pair], target.at[0])
        for source, target in ((k_hbm, k_ref), (v_hbm, v_ref), (q_hbm, q_ref), (g_hbm, g_ref))
    ]
    copies = [pltpu.make_async_copy(source, target, sems.at[i]) for i, (source, target) in enumerate(moves)]
    for copy in copies:
        copy.start()
    rows = q_ref.shape[1]
    copies[0].wait()
    copies[1].wait()
    reach = jnp.zeros((), jnp.int32)
    for first in range(0, doc_ref.shape[1], rows):
        reach = jnp.maximum(
            reach, first - jnp.min(jnp.maximum(doc_ref[:, first : first + rows], win_ref[:, first : first + rows]))
        )
    size_ref[0] = jnp.clip((reach + BLK - 1) // BLK, FEWEST, WBLK - 1) - FEWEST
    first_row = pl.multiple_of(lax.axis_index("ctx") * rows, BLK)
    seq_index = lax.axis_index("dp") * pl.num_programs(0) // HEADS
    own = (pl.ds(seq_index, 1), pl.ds(first_row, rows))
    low_ref[...] = jnp.maximum(doc_ref[own], win_ref[own]) - first_row
    for copy in copies[2:]:
        copy.wait()


def own_stats_kernel(
    q_ref, k_ref, v_ref, g_ref, gain_ref, low_ref,
    scaled_ref, keyt_ref, stats_ref, weight_ref, slope_ref, *, factor,
):
    rows = q_ref.shape[1]
    keyt_ref[0] = k_ref[0].T
    scaled_ref[0] = (q_ref[0].astype(jnp.float32) * gain_ref[0]).astype(jnp.bfloat16)
    for start, stop in groups(rows):
        logits = mm_t(k_ref[0, :stop, :], scaled_ref[0, start:stop, :]) * factor
        key_at = lax.broadcasted_iota(jnp.int32, logits.shape, 0)
        query_at = start + lax.broadcasted_iota(jnp.int32, logits.shape, 1)
        visible = (key_at >= low_ref[:, start:stop]) & (key_at <= query_at)
        logits = jnp.where(visible, logits, NEG)
        top = jnp.max(logits, axis=0, keepdims=True)
        weights = jnp.exp2(logits - top)
        slopes = mm_t(v_ref[0, :stop, :], g_ref[0, start:stop, :])
        weight_ref[0, :stop, start:stop] = weights
        slope_ref[0, :stop, start:stop] = slopes
        stats_ref[0, M_ROW : M_ROW + 1, start:stop] = top
        stats_ref[0, L_ROW : L_ROW + 1, start:stop] = jnp.sum(weights, axis=0, keepdims=True)
        stats_ref[0, D_ROW : D_ROW + 1, start:stop] = jnp.sum(weights * slopes, axis=0, keepdims=True)


def probs_kernel(
    scaled_ref, g_ref, low_ref, part_ref, weight_ref, kh_ref,
    delta_ref, hprobs_ref, probs_ref, dv_ref, *, factor,
):
    rows = scaled_ref.shape[1]
    halo = kh_ref.shape[1]
    for start, stop in groups(rows):
        own_top = part_ref[0, M_ROW : M_ROW + 1, start:stop]
        total = part_ref[0, L_ROW : L_ROW + 1, start:stop]
        if start < PREV:
            first = halo_from(start, halo)
            logits = mm_t(kh_ref[0, first:, :], scaled_ref[0, start:stop, :]) * factor
            key_at = (first - halo) + lax.broadcasted_iota(jnp.int32, logits.shape, 0)
            query_block = start + lax.broadcasted_iota(jnp.int32, (1, stop - start), 1) & -BLK
            lowest = jnp.maximum(low_ref[:, start:stop], query_block - PREV)
            logits = jnp.where(key_at >= lowest, logits, NEG)
            top = jnp.maximum(own_top, jnp.max(logits, axis=0, keepdims=True))
            weights = jnp.exp2(logits - top)
            shrink = jnp.exp2(own_top - top)
            total = total * shrink + jnp.sum(weights, axis=0, keepdims=True)
            inverse = 1.0 / total
            hprobs_ref[0, first:, start:stop] = (weights * inverse).astype(jnp.bfloat16)
            share = shrink * inverse
        else:
            share = 1.0 / total
        delta_ref[0, 0:1, start:stop] = part_ref[0, D_ROW : D_ROW + 1, start:stop] * share
        probs_ref[0, :stop, start:stop] = (weight_ref[0, :stop, start:stop] * share).astype(jnp.bfloat16)
    for first, last, seen in halo_chunks(halo, rows):
        dv_ref[0, first:last, :] = mm(hprobs_ref[0, first:last, :seen], g_ref[0, :seen, :]).astype(jnp.bfloat16)


def grads_kernel(
    q_ref, scaled_ref, g_ref, keyt_ref, part_ref, hprobs_ref, probs_ref, slope_ref, kh_ref, vh_ref,
    dq_ref, dk_ref, head_ref, grads_ref, hgrads_ref, *, score_scale,
):
    rows = q_ref.shape[1]
    halo = kh_ref.shape[1]
    halo_cols = kh_ref[0].T
    head_sum = jnp.zeros((1, q_ref.shape[2]), jnp.float32)
    for start, stop in groups(rows):
        delta = part_ref[0, 0:1, start:stop]
        if start < PREV:
            first = halo_from(start, halo)
            probs = hprobs_ref[0, first:, start:stop].astype(jnp.float32)
            slopes = mm_t(vh_ref[0, first:, :], g_ref[0, start:stop, :])
            delta = delta + jnp.sum(probs * slopes, axis=0, keepdims=True)
            hgrads = (probs * (slopes - delta)).astype(jnp.bfloat16)
            hgrads_ref[first:, start:stop] = hgrads
        probs = probs_ref[0, :stop, start:stop].astype(jnp.float32)
        grads = (probs * (slope_ref[0, :stop, start:stop] - delta)).astype(jnp.bfloat16)
        grads_ref[0, :stop, start:stop] = grads
        dq = mm(keyt_ref[0, :, :stop], grads)
        if start < PREV:
            dq = dq + mm(halo_cols[:, first:], hgrads)
        dq = dq.T * score_scale
        dq_ref[0, start:stop, :] = dq
        head_sum = head_sum + jnp.sum(dq * q_ref[0, start:stop, :].astype(jnp.float32), axis=0, keepdims=True)
    head_ref[0] = head_sum
    rest = head_sum
    riders = []
    for _ in range(3):
        riders.append(rest.astype(jnp.bfloat16))
        rest = rest - riders[-1].astype(jnp.float32)
    filler = jnp.zeros((RIDERS - 3, head_sum.shape[1]), jnp.bfloat16)
    dk_ref[0, halo:, :] = jnp.concatenate(riders + [filler], axis=0)
    for first, last, seen in halo_chunks(halo, rows):
        dk_ref[0, first:last, :] = (mm(hgrads_ref[first:last, :seen], scaled_ref[0, :seen, :]) * score_scale).astype(
            jnp.bfloat16
        )


def own_keys_kernel(
    g_ref, scaled_ref, probs_ref, grads_ref, dq_ref, gain_ref, back_ref, gq_ref, dv_ref, dk_ref, *, score_scale
):
    rows = g_ref.shape[1]
    gq_ref[0] = (dq_ref[0] * gain_ref[0]).astype(jnp.bfloat16)
    lead = rows - back_ref.shape[1]
    for first, last in groups(rows):
        own = mm(probs_ref[0, first:last, first:], g_ref[0, first:, :])
        cut = min(max(lead - first, 0), last - first)
        if cut:
            dv_ref[0, first : first + cut, :] = own[:cut].astype(jnp.bfloat16)
        if cut < last - first:
            back = back_ref[0, first + cut - lead : last - lead, :].astype(jnp.float32)
            dv_ref[0, first + cut : last, :] = (own[cut:] + back).astype(jnp.bfloat16)
        dk_ref[0, first:last, :] = mm(grads_ref[0, first:last, first:], scaled_ref[0, first:, :]) * score_scale


def finish_kernel(own_ref, back_ref, *refs, riding):
    terms, (dk_ref, gain_ref) = refs[:-2], refs[-2:]
    halo = back_ref.shape[1] - RIDERS
    lead = own_ref.shape[1] - halo
    if lead:
        dk_ref[0, :lead, :] = own_ref[0, :lead, :].astype(jnp.bfloat16)
    dk_ref[0, lead:, :] = (own_ref[0, lead:, :] + back_ref[0, :halo, :].astype(jnp.float32)).astype(jnp.bfloat16)
    total = terms[0][0]
    for term in terms[1:]:
        total = total + term[0]
    if riding:
        total = total + jnp.sum(back_ref[0, halo:, :].astype(jnp.float32), axis=0, keepdims=True)
    gain_ref[0] = total


def whole(shape):
    return pl.BlockSpec((1,) + shape, lambda p: (p,) + (0,) * len(shape))


def call(kernel, pair_count, in_specs, outs, weight, scratch=(), **fixed):
    specs, shapes = zip(*outs)
    return pl.pallas_call(
        functools.partial(kernel, **fixed),
        grid=(pair_count,),
        in_specs=in_specs,
        out_specs=specs,
        out_shape=shapes,
        scratch_shapes=list(scratch),
        compiler_params=pltpu.CompilerParams(vmem_limit_bytes=32 * 1024 * 1024),
        cost_estimate=pl.CostEstimate(flops=weight, bytes_accessed=1, transcendentals=0),
    )


def band(halo, aligned, keys_in, values_in, queries_in, grad_in, lower, gain_rows):
    pair_count, rows, width = queries_in.shape
    score_scale = 1.0 / math.sqrt(width)
    factor = score_scale * LOG2E
    bf16, f32 = jnp.bfloat16, jnp.float32
    key_halo = shift(keys_in[:, rows - halo :], "ctx", 1)
    value_halo = shift(values_in[:, rows - halo :], "ctx", 1)

    row_spec = whole((rows, width))
    gain_spec = whole((1, width))
    stat_spec = whole((8, rows))
    delta_spec = whole((1, rows))
    halo_spec = whole((halo, width))
    ridden_spec = whole((halo + RIDERS, width))
    keyt_spec = whole((width, rows))
    own_sq = whole((rows, rows))
    halo_sq = whole((halo, rows))
    low_spec = pl.BlockSpec((1, rows), lambda p: (0, 0))

    def shaped(shape, dtype):
        return jax.ShapeDtypeStruct((pair_count,) + shape, dtype)

    row_out = (row_spec, shaped((rows, width), bf16))
    wide_out = (row_spec, shaped((rows, width), f32))
    scaled, key_cols, part, own_weights, own_slopes = call(
        own_stats_kernel,
        pair_count,
        [row_spec] * 4 + [gain_spec, low_spec],
        (
            row_out,
            (keyt_spec, shaped((width, rows), bf16)),
            (stat_spec, shaped((8, rows), f32)),
            (own_sq, shaped((rows, rows), f32)),
            (own_sq, shaped((rows, rows), f32)),
        ),
        LIGHT,
        factor=factor,
    )(queries_in, keys_in, values_in, grad_in, gain_rows, lower)

    own_delta, halo_probs, own_probs, dv_halo = call(
        probs_kernel,
        pair_count,
        [row_spec, row_spec, low_spec, stat_spec, own_sq, halo_spec],
        (
            (delta_spec, shaped((1, rows), f32)),
            (halo_sq, shaped((halo, rows), bf16)),
            (own_sq, shaped((rows, rows), bf16)),
            (halo_spec, shaped((halo, width), bf16)),
        ),
        LIGHT,
        factor=factor,
    )(scaled, grad_in, lower, part, own_weights, key_halo)
    dv_back = shift(dv_halo, "ctx", -1)

    dq, dk_halo, head_terms, own_grads = call(
        grads_kernel,
        pair_count,
        [row_spec] * 3 + [keyt_spec, delta_spec, halo_sq, own_sq, own_sq, halo_spec, halo_spec],
        (
            wide_out,
            (ridden_spec, shaped((halo + RIDERS, width), bf16)),
            (gain_spec, shaped((1, width), f32)),
            (own_sq, shaped((rows, rows), bf16)),
        ),
        HEAVY,
        scratch=[pltpu.VMEM((halo, rows), bf16)],
        score_scale=score_scale,
    )(
        queries_in, scaled, grad_in, key_cols, own_delta, halo_probs, own_probs, own_slopes,
        key_halo, value_halo,
    )
    dk_back = shift(dk_halo, "ctx", -1)
    length = lax.axis_size("ctx")
    riding = aligned and 1 < length <= 4
    terms = [head_terms]
    if riding:
        terms += [shift(head_terms, "ctx", by) for by in range(1, length - 1)]
    elif aligned:
        terms = [lax.psum(head_terms, "ctx")]

    grad_queries, grad_values, dk_own = call(
        own_keys_kernel,
        pair_count,
        [row_spec, row_spec, own_sq, own_sq, row_spec, gain_spec, halo_spec],
        (row_out, row_out, wide_out),
        10**9,
        score_scale=score_scale,
    )(grad_in, scaled, own_probs, own_grads, dq, gain_rows, dv_back)
    grad_keys, gain_sum = call(
        finish_kernel,
        pair_count,
        [row_spec, ridden_spec] + [gain_spec] * len(terms),
        (row_out, (gain_spec, shaped((1, width), f32))),
        LIGHT,
        riding=riding,
    )(dk_own, dk_back, *terms)
    return grad_queries, grad_keys, grad_values, gain_sum


def on_device(queries, keys, values, grad_out, gain, doc_start, win_start):
    pair_count, rows, width = queries.shape
    head_first = lax.axis_index("dp") * pair_count % HEADS
    aligned = lax.axis_size("dp") * pair_count == HEADS and gain.shape[0] == pair_count * width
    if aligned:
        gain_rows = gain.reshape(pair_count, 1, width)
    else:
        full_gain = lax.all_gather(gain, "dp", axis=0, tiled=True)
        gain_rows = lax.dynamic_slice_in_dim(
            full_gain.reshape(HEADS, width), head_first, pair_count, 0
        ).reshape(pair_count, 1, width)

    hbm = pl.BlockSpec(memory_space=pltpu.HBM)
    row_out = (whole((rows, width)), jax.ShapeDtypeStruct((pair_count, rows, width), jnp.bfloat16))
    *loaded, size = call(
        load_kernel,
        pair_count,
        [hbm] * 6,
        [row_out] * 4
        + [
            (pl.BlockSpec((1, rows), lambda p: (0, 0)), jax.ShapeDtypeStruct((1, rows), jnp.int32)),
            (pl.BlockSpec(memory_space=pltpu.SMEM), jax.ShapeDtypeStruct((1,), jnp.int32)),
        ],
        LIGHT,
        scratch=[pltpu.VMEM(doc_start.shape, jnp.int32)] * 2 + [pltpu.SemaphoreType.DMA((6,))],
    )(*(pltpu.with_memory_space_constraint(x, pltpu.HBM) for x in (doc_start, win_start, keys, values, queries, grad_out)))
    grad_queries, grad_keys, grad_values, gain_sum = lax.switch(
        size[0],
        [functools.partial(band, blocks * BLK, aligned) for blocks in range(FEWEST, WBLK)],
        *loaded, gain_rows,
    )
    if aligned:
        grad_gain = gain_sum.reshape(pair_count * width)
    else:
        gain_table = lax.dynamic_update_slice_in_dim(
            jnp.zeros((HEADS, width), jnp.float32), gain_sum.reshape(pair_count, width), head_first, 0
        ).reshape(HEADS * width)
        everything = lax.psum(gain_table, ("ctx", "dp"))
        share = gain.shape[0]
        grad_gain = lax.dynamic_slice_in_dim(everything, lax.axis_index("dp") * share, share, 0)
    return (grad_queries, grad_keys, grad_values, grad_gain)


def solution(mesh):
    rows = P("dp", "ctx", None)
    return jax.shard_map(
        on_device,
        mesh=mesh,
        in_specs=(rows, rows, rows, rows, P("dp"), P(), P()),
        out_specs=(rows, rows, rows, P("dp")),
        check_vma=False,
    )
```

```python
import functools
import math

import jax
import jax.numpy as jnp
from jax import lax
from jax.experimental import pallas as pl
from jax.experimental.pallas import tpu as pltpu
from jax.sharding import PartitionSpec as P

HEADS = 8
BLK = 128
WBLK = 8
PREV = (WBLK - 1) * BLK
GROUP = 2 * BLK
LOG2E = 1.4426950408889634
NEG = -1e30
M_ROW, L_ROW, D_ROW = 0, 1, 2
LIGHT, HEAVY = 1, 10**10
FEWEST = 4
RIDERS = 16


def shift(value, axis, by):
    length = lax.axis_size(axis)
    pairs = [(i, (i + by) % length) for i in range(length)]
    return lax.ppermute(value, axis, pairs)


def mm(left, right):
    return lax.dot_general(left, right, (((1,), (0,)), ((), ())), preferred_element_type=jnp.float32)


def mm_t(left, right):
    return lax.dot_general(left, right, (((1,), (1,)), ((), ())), preferred_element_type=jnp.float32)


def groups(rows):
    return [(start, min(start + GROUP, rows)) for start in range(0, rows, GROUP)]


def halo_chunks(halo, rows):
    ahead = PREV - halo
    return [
        (max(0, start - ahead), min(halo, stop - ahead), min(stop, PREV))
        for start, stop in groups(rows)
        if start < PREV and stop > ahead
    ]


def halo_from(start, halo):
    return max(0, start - (PREV - halo))


def load_kernel(
    doc_hbm, win_hbm, k_hbm, v_hbm, q_hbm, g_hbm,
    k_ref, v_ref, q_ref, g_ref, low_ref, size_ref, doc_ref, win_ref, sems,
):
    pair = pl.program_id(0)
    moves = [(doc_hbm, doc_ref), (win_hbm, win_ref)]
    moves += [
        (source.at[pair], target.at[0])
        for source, target in ((k_hbm, k_ref), (v_hbm, v_ref), (q_hbm, q_ref), (g_hbm, g_ref))
    ]
    copies = [pltpu.make_async_copy(source, target, sems.at[i]) for i, (source, target) in enumerate(moves)]
    for copy in copies:
        copy.start()
    rows = q_ref.shape[1]
    copies[0].wait()
    copies[1].wait()
    reach = jnp.zeros((), jnp.int32)
    for first in range(0, doc_ref.shape[1], rows):
        reach = jnp.maximum(
            reach, first - jnp.min(jnp.maximum(doc_ref[:, first : first + rows], win_ref[:, first : first + rows]))
        )
    size_ref[0] = jnp.clip((reach + BLK - 1) // BLK, FEWEST, WBLK - 1) - FEWEST
    first_row = pl.multiple_of(lax.axis_index("ctx") * rows, BLK)
    seq_index = lax.axis_index("dp") * pl.num_programs(0) // HEADS
    own = (pl.ds(seq_index, 1), pl.ds(first_row, rows))
    low_ref[...] = jnp.maximum(doc_ref[own], win_ref[own]) - first_row
    for copy in copies[2:]:
        copy.wait()


def own_stats_kernel(
    q_ref, k_ref, v_ref, g_ref, gain_ref, low_ref,
    scaled_ref, keyt_ref, stats_ref, weight_ref, slope_ref, *, factor,
):
    rows = q_ref.shape[1]
    keyt_ref[0] = k_ref[0].T
    scaled_ref[0] = (q_ref[0].astype(jnp.float32) * gain_ref[0]).astype(jnp.bfloat16)

    @pl.loop(0, rows // GROUP)
    def _(group):
        own = pl.ds(pl.multiple_of(group * GROUP, GROUP), GROUP)
        logits = mm_t(k_ref[0], scaled_ref[0, own, :]) * factor
        key_at = lax.broadcasted_iota(jnp.int32, logits.shape, 0)
        query_at = group * GROUP + lax.broadcasted_iota(jnp.int32, (1, GROUP), 1)
        visible = (key_at >= low_ref[:, own]) & (key_at <= query_at)
        logits = jnp.where(visible, logits, NEG)
        top = jnp.max(logits, axis=0, keepdims=True)
        weights = jnp.exp2(logits - top)
        slopes = mm_t(v_ref[0], g_ref[0, own, :])
        weight_ref[0, :, own] = weights
        slope_ref[0, :, own] = slopes
        stats_ref[0, M_ROW : M_ROW + 1, own] = top
        stats_ref[0, L_ROW : L_ROW + 1, own] = jnp.sum(weights, axis=0, keepdims=True)
        stats_ref[0, D_ROW : D_ROW + 1, own] = jnp.sum(weights * slopes, axis=0, keepdims=True)


def probs_kernel(
    scaled_ref, g_ref, low_ref, part_ref, weight_ref, kh_ref,
    delta_ref, hprobs_ref, probs_ref, dv_ref, *, factor,
):
    rows = scaled_ref.shape[1]
    halo = kh_ref.shape[1]
    for start, stop in groups(rows):
        own_top = part_ref[0, M_ROW : M_ROW + 1, start:stop]
        total = part_ref[0, L_ROW : L_ROW + 1, start:stop]
        if start < PREV:
            first = halo_from(start, halo)
            logits = mm_t(kh_ref[0, first:, :], scaled_ref[0, start:stop, :]) * factor
            key_at = (first - halo) + lax.broadcasted_iota(jnp.int32, logits.shape, 0)
            query_block = start + lax.broadcasted_iota(jnp.int32, (1, stop - start), 1) & -BLK
            lowest = jnp.maximum(low_ref[:, start:stop], query_block - PREV)
            logits = jnp.where(key_at >= lowest, logits, NEG)
            top = jnp.maximum(own_top, jnp.max(logits, axis=0, keepdims=True))
            weights = jnp.exp2(logits - top)
            shrink = jnp.exp2(own_top - top)
            total = total * shrink + jnp.sum(weights, axis=0, keepdims=True)
            inverse = 1.0 / total
            hprobs_ref[0, first:, start:stop] = (weights * inverse).astype(jnp.bfloat16)
            share = shrink * inverse
        else:
            share = 1.0 / total
        delta_ref[0, 0:1, start:stop] = part_ref[0, D_ROW : D_ROW + 1, start:stop] * share
        probs_ref[0, :stop, start:stop] = (weight_ref[0, :stop, start:stop] * share).astype(jnp.bfloat16)
        if stop < rows:
            probs_ref[0, stop:, start:stop] = jnp.zeros((rows - stop, stop - start), jnp.bfloat16)
    for first, last, seen in halo_chunks(halo, rows):
        dv_ref[0, first:last, :] = mm(hprobs_ref[0, first:last, :seen], g_ref[0, :seen, :]).astype(jnp.bfloat16)


def grads_kernel(
    q_ref, scaled_ref, g_ref, keyt_ref, part_ref, hprobs_ref, probs_ref, slope_ref, kh_ref, vh_ref,
    dq_ref, dk_ref, head_ref, grads_ref, hgrads_ref, *, score_scale,
):
    rows = q_ref.shape[1]
    halo = kh_ref.shape[1]
    halo_cols = kh_ref[0].T
    head_sum = jnp.zeros((1, q_ref.shape[2]), jnp.float32)
    for start, stop in groups(rows):
        delta = part_ref[0, 0:1, start:stop]
        if start < PREV:
            first = halo_from(start, halo)
            probs = hprobs_ref[0, first:, start:stop].astype(jnp.float32)
            slopes = mm_t(vh_ref[0, first:, :], g_ref[0, start:stop, :])
            delta = delta + jnp.sum(probs * slopes, axis=0, keepdims=True)
            hgrads = (probs * (slopes - delta)).astype(jnp.bfloat16)
            hgrads_ref[first:, start:stop] = hgrads
        probs = probs_ref[0, :stop, start:stop].astype(jnp.float32)
        grads = (probs * (slope_ref[0, :stop, start:stop] - delta)).astype(jnp.bfloat16)
        grads_ref[0, :stop, start:stop] = grads
        if stop < rows:
            grads_ref[0, stop:, start:stop] = jnp.zeros((rows - stop, stop - start), jnp.bfloat16)
        dq = mm(keyt_ref[0, :, :stop], grads)
        if start < PREV:
            dq = dq + mm(halo_cols[:, first:], hgrads)
        dq = dq.T * score_scale
        dq_ref[0, start:stop, :] = dq
        head_sum = head_sum + jnp.sum(dq * q_ref[0, start:stop, :].astype(jnp.float32), axis=0, keepdims=True)
    head_ref[0] = head_sum
    rest = head_sum
    riders = []
    for _ in range(3):
        riders.append(rest.astype(jnp.bfloat16))
        rest = rest - riders[-1].astype(jnp.float32)
    filler = jnp.zeros((RIDERS - 3, head_sum.shape[1]), jnp.bfloat16)
    dk_ref[0, halo:, :] = jnp.concatenate(riders + [filler], axis=0)
    for first, last, seen in halo_chunks(halo, rows):
        dk_ref[0, first:last, :] = (mm(hgrads_ref[first:last, :seen], scaled_ref[0, :seen, :]) * score_scale).astype(
            jnp.bfloat16
        )


def own_keys_kernel(
    g_ref, scaled_ref, probs_ref, grads_ref, dq_ref, gain_ref, back_ref, gq_ref, dv_ref, dk_ref, dsum_ref, *, score_scale
):
    rows = g_ref.shape[1]
    gq_ref[0] = (dq_ref[0] * gain_ref[0]).astype(jnp.bfloat16)
    lead = rows - back_ref.shape[1]

    @pl.loop(0, rows // GROUP)
    def _(group):
        own = pl.ds(pl.multiple_of(group * GROUP, GROUP), GROUP)
        dsum_ref[own, :] = mm(probs_ref[0, own, :], g_ref[0])
        dk_ref[0, own, :] = mm(grads_ref[0, own, :], scaled_ref[0]) * score_scale

    if lead:
        dv_ref[0, :lead, :] = dsum_ref[:lead, :].astype(jnp.bfloat16)
    dv_ref[0, lead:, :] = (dsum_ref[lead:, :] + back_ref[0].astype(jnp.float32)).astype(jnp.bfloat16)


def finish_kernel(own_ref, back_ref, *refs, riding):
    terms, (dk_ref, gain_ref) = refs[:-2], refs[-2:]
    halo = back_ref.shape[1] - RIDERS
    lead = own_ref.shape[1] - halo
    if lead:
        dk_ref[0, :lead, :] = own_ref[0, :lead, :].astype(jnp.bfloat16)
    dk_ref[0, lead:, :] = (own_ref[0, lead:, :] + back_ref[0, :halo, :].astype(jnp.float32)).astype(jnp.bfloat16)
    total = terms[0][0]
    for term in terms[1:]:
        total = total + term[0]
    if riding:
        total = total + jnp.sum(back_ref[0, halo:, :].astype(jnp.float32), axis=0, keepdims=True)
    gain_ref[0] = total


def whole(shape):
    return pl.BlockSpec((1,) + shape, lambda p: (p,) + (0,) * len(shape))


def call(kernel, pair_count, in_specs, outs, weight, scratch=(), **fixed):
    specs, shapes = zip(*outs)
    return pl.pallas_call(
        functools.partial(kernel, **fixed),
        grid=(pair_count,),
        in_specs=in_specs,
        out_specs=specs,
        out_shape=shapes,
        scratch_shapes=list(scratch),
        compiler_params=pltpu.CompilerParams(vmem_limit_bytes=32 * 1024 * 1024),
        cost_estimate=pl.CostEstimate(flops=weight, bytes_accessed=1, transcendentals=0),
    )


def band(halo, aligned, keys_in, values_in, queries_in, grad_in, lower, gain_rows):
    pair_count, rows, width = queries_in.shape
    score_scale = 1.0 / math.sqrt(width)
    factor = score_scale * LOG2E
    bf16, f32 = jnp.bfloat16, jnp.float32
    key_halo = shift(keys_in[:, rows - halo :], "ctx", 1)
    value_halo = shift(values_in[:, rows - halo :], "ctx", 1)

    row_spec = whole((rows, width))
    gain_spec = whole((1, width))
    stat_spec = whole((8, rows))
    delta_spec = whole((1, rows))
    halo_spec = whole((halo, width))
    ridden_spec = whole((halo + RIDERS, width))
    keyt_spec = whole((width, rows))
    own_sq = whole((rows, rows))
    halo_sq = whole((halo, rows))
    low_spec = pl.BlockSpec((1, rows), lambda p: (0, 0))

    def shaped(shape, dtype):
        return jax.ShapeDtypeStruct((pair_count,) + shape, dtype)

    row_out = (row_spec, shaped((rows, width), bf16))
    wide_out = (row_spec, shaped((rows, width), f32))
    scaled, key_cols, part, own_weights, own_slopes = call(
        own_stats_kernel,
        pair_count,
        [row_spec] * 4 + [gain_spec, low_spec],
        (
            row_out,
            (keyt_spec, shaped((width, rows), bf16)),
            (stat_spec, shaped((8, rows), f32)),
            (own_sq, shaped((rows, rows), f32)),
            (own_sq, shaped((rows, rows), f32)),
        ),
        LIGHT,
        factor=factor,
    )(queries_in, keys_in, values_in, grad_in, gain_rows, lower)

    own_delta, halo_probs, own_probs, dv_halo = call(
        probs_kernel,
        pair_count,
        [row_spec, row_spec, low_spec, stat_spec, own_sq, halo_spec],
        (
            (delta_spec, shaped((1, rows), f32)),
            (halo_sq, shaped((halo, rows), bf16)),
            (own_sq, shaped((rows, rows), bf16)),
            (halo_spec, shaped((halo, width), bf16)),
        ),
        LIGHT,
        factor=factor,
    )(scaled, grad_in, lower, part, own_weights, key_halo)
    dv_back = shift(dv_halo, "ctx", -1)

    dq, dk_halo, head_terms, own_grads = call(
        grads_kernel,
        pair_count,
        [row_spec] * 3 + [keyt_spec, delta_spec, halo_sq, own_sq, own_sq, halo_spec, halo_spec],
        (
            wide_out,
            (ridden_spec, shaped((halo + RIDERS, width), bf16)),
            (gain_spec, shaped((1, width), f32)),
            (own_sq, shaped((rows, rows), bf16)),
        ),
        HEAVY,
        scratch=[pltpu.VMEM((halo, rows), bf16)],
        score_scale=score_scale,
    )(
        queries_in, scaled, grad_in, key_cols, own_delta, halo_probs, own_probs, own_slopes,
        key_halo, value_halo,
    )
    dk_back = shift(dk_halo, "ctx", -1)
    length = lax.axis_size("ctx")
    riding = aligned and 1 < length <= 4
    terms = [head_terms]
    if riding:
        terms += [shift(head_terms, "ctx", by) for by in range(1, length - 1)]
    elif aligned:
        terms = [lax.psum(head_terms, "ctx")]

    grad_queries, grad_values, dk_own = call(
        own_keys_kernel,
        pair_count,
        [row_spec, row_spec, own_sq, own_sq, row_spec, gain_spec, halo_spec],
        (row_out, row_out, wide_out),
        10**9,
        scratch=[pltpu.VMEM((rows, width), f32)],
        score_scale=score_scale,
    )(grad_in, scaled, own_probs, own_grads, dq, gain_rows, dv_back)
    grad_keys, gain_sum = call(
        finish_kernel,
        pair_count,
        [row_spec, ridden_spec] + [gain_spec] * len(terms),
        (row_out, (gain_spec, shaped((1, width), f32))),
        LIGHT,
        riding=riding,
    )(dk_own, dk_back, *terms)
    return grad_queries, grad_keys, grad_values, gain_sum


def on_device(queries, keys, values, grad_out, gain, doc_start, win_start):
    pair_count, rows, width = queries.shape
    head_first = lax.axis_index("dp") * pair_count % HEADS
    aligned = lax.axis_size("dp") * pair_count == HEADS and gain.shape[0] == pair_count * width
    if aligned:
        gain_rows = gain.reshape(pair_count, 1, width)
    else:
        full_gain = lax.all_gather(gain, "dp", axis=0, tiled=True)
        gain_rows = lax.dynamic_slice_in_dim(
            full_gain.reshape(HEADS, width), head_first, pair_count, 0
        ).reshape(pair_count, 1, width)

    hbm = pl.BlockSpec(memory_space=pltpu.HBM)
    row_out = (whole((rows, width)), jax.ShapeDtypeStruct((pair_count, rows, width), jnp.bfloat16))
    *loaded, size = call(
        load_kernel,
        pair_count,
        [hbm] * 6,
        [row_out] * 4
        + [
            (pl.BlockSpec((1, rows), lambda p: (0, 0)), jax.ShapeDtypeStruct((1, rows), jnp.int32)),
            (pl.BlockSpec(memory_space=pltpu.SMEM), jax.ShapeDtypeStruct((1,), jnp.int32)),
        ],
        LIGHT,
        scratch=[pltpu.VMEM(doc_start.shape, jnp.int32)] * 2 + [pltpu.SemaphoreType.DMA((6,))],
    )(*(pltpu.with_memory_space_constraint(x, pltpu.HBM) for x in (doc_start, win_start, keys, values, queries, grad_out)))
    grad_queries, grad_keys, grad_values, gain_sum = lax.switch(
        size[0],
        [functools.partial(band, blocks * BLK, aligned) for blocks in range(FEWEST, WBLK)],
        *loaded, gain_rows,
    )
    if aligned:
        grad_gain = gain_sum.reshape(pair_count * width)
    else:
        gain_table = lax.dynamic_update_slice_in_dim(
            jnp.zeros((HEADS, width), jnp.float32), gain_sum.reshape(pair_count, width), head_first, 0
        ).reshape(HEADS * width)
        everything = lax.psum(gain_table, ("ctx", "dp"))
        share = gain.shape[0]
        grad_gain = lax.dynamic_slice_in_dim(everything, lax.axis_index("dp") * share, share, 0)
    return (grad_queries, grad_keys, grad_values, grad_gain)


def solution(mesh):
    rows = P("dp", "ctx", None)
    return jax.shard_map(
        on_device,
        mesh=mesh,
        in_specs=(rows, rows, rows, rows, P("dp"), P(), P()),
        out_specs=(rows, rows, rows, P("dp")),
        check_vma=False,
    )
```

```python
import functools
import math

import jax
import jax.numpy as jnp
from jax import lax
from jax.experimental import pallas as pl
from jax.experimental.pallas import tpu as pltpu
from jax.sharding import PartitionSpec as P

HEADS = 8
BLK = 128
WBLK = 8
PREV = (WBLK - 1) * BLK
GROUP = 2 * BLK
LOG2E = 1.4426950408889634
NEG = -1e30
M_ROW, L_ROW, D_ROW = 0, 1, 2
LIGHT, HEAVY = 1, 10**10
FEWEST = 4
LONG = 5
RIDERS = 16


def shift(value, axis, by):
    length = lax.axis_size(axis)
    pairs = [(i, (i + by) % length) for i in range(length)]
    return lax.ppermute(value, axis, pairs)


def mm(left, right):
    return lax.dot_general(left, right, (((1,), (0,)), ((), ())), preferred_element_type=jnp.float32)


def mm_t(left, right):
    return lax.dot_general(left, right, (((1,), (1,)), ((), ())), preferred_element_type=jnp.float32)


def groups(rows):
    return [(start, min(start + GROUP, rows)) for start in range(0, rows, GROUP)]


def halo_chunks(halo, rows):
    ahead = PREV - halo
    return [
        (max(0, start - ahead), min(halo, stop - ahead), min(stop, PREV))
        for start, stop in groups(rows)
        if start < PREV and stop > ahead
    ]


def halo_from(start, halo):
    return max(0, start - (PREV - halo))


def load_kernel(
    doc_hbm, win_hbm, k_hbm, v_hbm, q_hbm, g_hbm,
    k_ref, v_ref, q_ref, g_ref, low_ref, size_ref, doc_ref, win_ref, sems,
):
    pair = pl.program_id(0)
    moves = [(doc_hbm, doc_ref), (win_hbm, win_ref)]
    moves += [
        (source.at[pair], target.at[0])
        for source, target in ((k_hbm, k_ref), (v_hbm, v_ref), (q_hbm, q_ref), (g_hbm, g_ref))
    ]
    copies = [pltpu.make_async_copy(source, target, sems.at[i]) for i, (source, target) in enumerate(moves)]
    for copy in copies:
        copy.start()
    rows = q_ref.shape[1]
    copies[0].wait()
    copies[1].wait()
    reach = jnp.zeros((), jnp.int32)
    for first in range(0, doc_ref.shape[1], rows):
        reach = jnp.maximum(
            reach, first - jnp.min(jnp.maximum(doc_ref[:, first : first + rows], win_ref[:, first : first + rows]))
        )
    size_ref[0] = jnp.clip((reach + BLK - 1) // BLK, FEWEST, WBLK - 1) - FEWEST
    first_row = pl.multiple_of(lax.axis_index("ctx") * rows, BLK)
    seq_index = lax.axis_index("dp") * pl.num_programs(0) // HEADS
    own = (pl.ds(seq_index, 1), pl.ds(first_row, rows))
    low_ref[...] = jnp.maximum(doc_ref[own], win_ref[own]) - first_row
    for copy in copies[2:]:
        copy.wait()


def own_stats_kernel(
    q_ref, k_ref, v_ref, g_ref, gain_ref, low_ref,
    scaled_ref, keyt_ref, stats_ref, weight_ref, slope_ref, *, factor, step,
):
    rows = q_ref.shape[1]
    keyt_ref[0] = k_ref[0].T
    scaled_ref[0] = (q_ref[0].astype(jnp.float32) * gain_ref[0]).astype(jnp.bfloat16)

    @pl.loop(0, rows // step)
    def _(group):
        own = pl.ds(pl.multiple_of(group * step, step), step)
        logits = mm_t(k_ref[0], scaled_ref[0, own, :]) * factor
        key_at = lax.broadcasted_iota(jnp.int32, logits.shape, 0)
        query_at = group * step + lax.broadcasted_iota(jnp.int32, (1, step), 1)
        visible = (key_at >= low_ref[:, own]) & (key_at <= query_at)
        logits = jnp.where(visible, logits, NEG)
        top = jnp.max(logits, axis=0, keepdims=True)
        weights = jnp.exp2(logits - top)
        slopes = mm_t(v_ref[0], g_ref[0, own, :])
        weight_ref[0, :, own] = weights
        slope_ref[0, :, own] = slopes
        stats_ref[0, M_ROW : M_ROW + 1, own] = top
        stats_ref[0, L_ROW : L_ROW + 1, own] = jnp.sum(weights, axis=0, keepdims=True)
        stats_ref[0, D_ROW : D_ROW + 1, own] = jnp.sum(weights * slopes, axis=0, keepdims=True)


def probs_kernel(
    scaled_ref, g_ref, low_ref, part_ref, weight_ref, kh_ref,
    delta_ref, hprobs_ref, probs_ref, dv_ref, share_ref, *, factor, step,
):
    rows = scaled_ref.shape[1]
    halo = kh_ref.shape[1]
    for start, stop in groups(rows):
        own_top = part_ref[0, M_ROW : M_ROW + 1, start:stop]
        total = part_ref[0, L_ROW : L_ROW + 1, start:stop]
        if start < PREV:
            first = halo_from(start, halo)
            logits = mm_t(kh_ref[0, first:, :], scaled_ref[0, start:stop, :]) * factor
            key_at = (first - halo) + lax.broadcasted_iota(jnp.int32, logits.shape, 0)
            query_block = start + lax.broadcasted_iota(jnp.int32, (1, stop - start), 1) & -BLK
            lowest = jnp.maximum(low_ref[:, start:stop], query_block - PREV)
            logits = jnp.where(key_at >= lowest, logits, NEG)
            top = jnp.maximum(own_top, jnp.max(logits, axis=0, keepdims=True))
            weights = jnp.exp2(logits - top)
            shrink = jnp.exp2(own_top - top)
            total = total * shrink + jnp.sum(weights, axis=0, keepdims=True)
            inverse = 1.0 / total
            hprobs_ref[0, first:, start:stop] = (weights * inverse).astype(jnp.bfloat16)
            share = shrink * inverse
        else:
            share = 1.0 / total
        delta_ref[0, 0:1, start:stop] = part_ref[0, D_ROW : D_ROW + 1, start:stop] * share
        share_ref[:, start:stop] = share

    @pl.loop(0, rows // step)
    def _(group):
        own = pl.ds(pl.multiple_of(group * step, step), step)
        probs_ref[0, :, own] = (weight_ref[0, :, own] * share_ref[:, own]).astype(jnp.bfloat16)

    for first, last, seen in halo_chunks(halo, rows):
        dv_ref[0, first:last, :] = mm(hprobs_ref[0, first:last, :seen], g_ref[0, :seen, :]).astype(jnp.bfloat16)


def riders_of(terms):
    riders = []
    for _ in range(3):
        riders.append(terms.astype(jnp.bfloat16))
        terms = terms - riders[-1].astype(jnp.float32)
    filler = jnp.zeros((RIDERS - 3, terms.shape[1]), jnp.bfloat16)
    return jnp.concatenate(riders + [filler], axis=0)


def grads_kernel(
    q_ref, scaled_ref, g_ref, keyt_ref, part_ref, hprobs_ref, probs_ref, slope_ref, kh_ref, vh_ref,
    dq_ref, dk_ref, head_ref, grads_ref, hgrads_ref, *, score_scale,
):
    rows = q_ref.shape[1]
    halo = kh_ref.shape[1]
    halo_cols = kh_ref[0].T
    head_sum = jnp.zeros((1, q_ref.shape[2]), jnp.float32)
    spans = groups(rows)
    deltas, halo_slopes = [], []
    for start, stop in spans:
        delta = part_ref[0, 0:1, start:stop]
        slopes = None
        if start < PREV:
            first = halo_from(start, halo)
            slopes = mm_t(vh_ref[0, first:, :], g_ref[0, start:stop, :])
            delta = delta + jnp.sum(hprobs_ref[0, first:, start:stop].astype(jnp.float32) * slopes, axis=0, keepdims=True)
        deltas.append(delta)
        halo_slopes.append(slopes)
    for (start, stop), delta, slopes in zip(spans, deltas, halo_slopes):
        if slopes is not None:
            first = halo_from(start, halo)
            hgrads_ref[first:, start:stop] = (
                hprobs_ref[0, first:, start:stop].astype(jnp.float32) * (slopes - delta)
            ).astype(jnp.bfloat16)
        probs = probs_ref[0, :stop, start:stop].astype(jnp.float32)
        grads_ref[0, :stop, start:stop] = (probs * (slope_ref[0, :stop, start:stop] - delta)).astype(jnp.bfloat16)
        if stop < rows:
            grads_ref[0, stop:, start:stop] = jnp.zeros((rows - stop, stop - start), jnp.bfloat16)
    for start, stop in spans:
        dq = mm(keyt_ref[0, :, :stop], grads_ref[0, :stop, start:stop])
        if start < PREV:
            first = halo_from(start, halo)
            dq = dq + mm(halo_cols[:, first:], hgrads_ref[first:, start:stop])
        dq = dq.T * score_scale
        dq_ref[0, start:stop, :] = dq
        head_sum = head_sum + jnp.sum(dq * q_ref[0, start:stop, :].astype(jnp.float32), axis=0, keepdims=True)
    head_ref[0] = head_sum
    dk_ref[0, halo:, :] = riders_of(head_sum)
    for first, last, seen in halo_chunks(halo, rows):
        dk_ref[0, first:last, :] = (mm(hgrads_ref[first:last, :seen], scaled_ref[0, :seen, :]) * score_scale).astype(
            jnp.bfloat16
        )


def own_keys_kernel(
    g_ref, scaled_ref, probs_ref, grads_ref, dq_ref, gain_ref, back_ref, gq_ref, dv_ref, dk_ref, dsum_ref, *, score_scale, step
):
    rows = g_ref.shape[1]
    gq_ref[0] = (dq_ref[0] * gain_ref[0]).astype(jnp.bfloat16)
    lead = rows - back_ref.shape[1]

    @pl.loop(0, rows // step)
    def _(group):
        own = pl.ds(pl.multiple_of(group * step, step), step)
        dsum_ref[own, :] = mm(probs_ref[0, own, :], g_ref[0])
        dk_ref[0, own, :] = mm(grads_ref[0, own, :], scaled_ref[0]) * score_scale

    if lead:
        dv_ref[0, :lead, :] = dsum_ref[:lead, :].astype(jnp.bfloat16)
    dv_ref[0, lead:, :] = (dsum_ref[lead:, :] + back_ref[0].astype(jnp.float32)).astype(jnp.bfloat16)


def finish_kernel(own_ref, back_ref, *refs, riding):
    terms, (dk_ref, gain_ref) = refs[:-2], refs[-2:]
    halo = back_ref.shape[1] - RIDERS
    lead = own_ref.shape[1] - halo
    if lead:
        dk_ref[0, :lead, :] = own_ref[0, :lead, :].astype(jnp.bfloat16)
    dk_ref[0, lead:, :] = (own_ref[0, lead:, :] + back_ref[0, :halo, :].astype(jnp.float32)).astype(jnp.bfloat16)
    total = terms[0][0]
    for term in terms[1:]:
        total = total + term[0]
    if riding:
        total = total + jnp.sum(back_ref[0, halo:, :].astype(jnp.float32), axis=0, keepdims=True)
    gain_ref[0] = total


def whole(shape):
    return pl.BlockSpec((1,) + shape, lambda p: (p,) + (0,) * len(shape))


def call(kernel, pair_count, in_specs, outs, weight, scratch=(), **fixed):
    specs, shapes = zip(*outs)
    return pl.pallas_call(
        functools.partial(kernel, **fixed),
        grid=(pair_count,),
        in_specs=in_specs,
        out_specs=specs,
        out_shape=shapes,
        scratch_shapes=list(scratch),
        compiler_params=pltpu.CompilerParams(vmem_limit_bytes=32 * 1024 * 1024),
        cost_estimate=pl.CostEstimate(flops=weight, bytes_accessed=1, transcendentals=0),
    )


def band(halo, aligned, keys_in, values_in, queries_in, grad_in, lower, gain_rows):
    pair_count, rows, width = queries_in.shape
    score_scale = 1.0 / math.sqrt(width)
    factor = score_scale * LOG2E
    bf16, f32 = jnp.bfloat16, jnp.float32
    key_halo = shift(keys_in[:, rows - halo :], "ctx", 1)
    value_halo = shift(values_in[:, rows - halo :], "ctx", 1)

    row_spec = whole((rows, width))
    gain_spec = whole((1, width))
    stat_spec = whole((8, rows))
    delta_spec = whole((1, rows))
    halo_spec = whole((halo, width))
    ridden_spec = whole((halo + RIDERS, width))
    keyt_spec = whole((width, rows))
    own_sq = whole((rows, rows))
    halo_sq = whole((halo, rows))
    low_spec = pl.BlockSpec((1, rows), lambda p: (0, 0))

    def shaped(shape, dtype):
        return jax.ShapeDtypeStruct((pair_count,) + shape, dtype)

    row_out = (row_spec, shaped((rows, width), bf16))
    wide_out = (row_spec, shaped((rows, width), f32))
    scaled, key_cols, part, own_weights, own_slopes = call(
        own_stats_kernel,
        pair_count,
        [row_spec] * 4 + [gain_spec, low_spec],
        (
            row_out,
            (keyt_spec, shaped((width, rows), bf16)),
            (stat_spec, shaped((8, rows), f32)),
            (own_sq, shaped((rows, rows), f32)),
            (own_sq, shaped((rows, rows), f32)),
        ),
        LIGHT,
        factor=factor,
        step=BLK if halo >= LONG * BLK else GROUP,
    )(queries_in, keys_in, values_in, grad_in, gain_rows, lower)

    own_delta, halo_probs, own_probs, dv_halo = call(
        probs_kernel,
        pair_count,
        [row_spec, row_spec, low_spec, stat_spec, own_sq, halo_spec],
        (
            (delta_spec, shaped((1, rows), f32)),
            (halo_sq, shaped((halo, rows), bf16)),
            (own_sq, shaped((rows, rows), bf16)),
            (halo_spec, shaped((halo, width), bf16)),
        ),
        LIGHT,
        scratch=[pltpu.VMEM((1, rows), f32)],
        factor=factor,
        step=GROUP,
    )(scaled, grad_in, lower, part, own_weights, key_halo)
    dv_back = shift(dv_halo, "ctx", -1)

    dq, dk_halo, head_terms, own_grads = call(
        grads_kernel,
        pair_count,
        [row_spec] * 3 + [keyt_spec, delta_spec, halo_sq, own_sq, own_sq, halo_spec, halo_spec],
        (
            wide_out,
            (ridden_spec, shaped((halo + RIDERS, width), bf16)),
            (gain_spec, shaped((1, width), f32)),
            (own_sq, shaped((rows, rows), bf16)),
        ),
        HEAVY,
        scratch=[pltpu.VMEM((halo, rows), bf16)],
        score_scale=score_scale,
    )(
        queries_in, scaled, grad_in, key_cols, own_delta, halo_probs, own_probs, own_slopes,
        key_halo, value_halo,
    )
    dk_back = shift(dk_halo, "ctx", -1)
    length = lax.axis_size("ctx")
    riding = aligned and 1 < length <= 4
    terms = [head_terms]
    if riding:
        terms += [shift(head_terms, "ctx", by) for by in range(1, length - 1)]
    elif aligned:
        terms = [lax.psum(head_terms, "ctx")]

    grad_queries, grad_values, dk_own = call(
        own_keys_kernel,
        pair_count,
        [row_spec, row_spec, own_sq, own_sq, row_spec, gain_spec, halo_spec],
        (row_out, row_out, wide_out),
        10**9,
        scratch=[pltpu.VMEM((rows, width), f32)],
        score_scale=score_scale,
        step=BLK if halo >= LONG * BLK else GROUP,
    )(grad_in, scaled, own_probs, own_grads, dq, gain_rows, dv_back)
    grad_keys, gain_sum = call(
        finish_kernel,
        pair_count,
        [row_spec, ridden_spec] + [gain_spec] * len(terms),
        (row_out, (gain_spec, shaped((1, width), f32))),
        LIGHT,
        riding=riding,
    )(dk_own, dk_back, *terms)
    return grad_queries, grad_keys, grad_values, gain_sum


def on_device(queries, keys, values, grad_out, gain, doc_start, win_start):
    pair_count, rows, width = queries.shape
    head_first = lax.axis_index("dp") * pair_count % HEADS
    aligned = lax.axis_size("dp") * pair_count == HEADS and gain.shape[0] == pair_count * width
    if aligned:
        gain_rows = gain.reshape(pair_count, 1, width)
    else:
        full_gain = lax.all_gather(gain, "dp", axis=0, tiled=True)
        gain_rows = lax.dynamic_slice_in_dim(
            full_gain.reshape(HEADS, width), head_first, pair_count, 0
        ).reshape(pair_count, 1, width)

    hbm = pl.BlockSpec(memory_space=pltpu.HBM)
    row_out = (whole((rows, width)), jax.ShapeDtypeStruct((pair_count, rows, width), jnp.bfloat16))
    *loaded, size = call(
        load_kernel,
        pair_count,
        [hbm] * 6,
        [row_out] * 4
        + [
            (pl.BlockSpec((1, rows), lambda p: (0, 0)), jax.ShapeDtypeStruct((1, rows), jnp.int32)),
            (pl.BlockSpec(memory_space=pltpu.SMEM), jax.ShapeDtypeStruct((1,), jnp.int32)),
        ],
        LIGHT,
        scratch=[pltpu.VMEM(doc_start.shape, jnp.int32)] * 2 + [pltpu.SemaphoreType.DMA((6,))],
    )(*(pltpu.with_memory_space_constraint(x, pltpu.HBM) for x in (doc_start, win_start, keys, values, queries, grad_out)))
    grad_queries, grad_keys, grad_values, gain_sum = lax.switch(
        size[0],
        [functools.partial(band, blocks * BLK, aligned) for blocks in range(FEWEST, WBLK)],
        *loaded, gain_rows,
    )
    if aligned:
        grad_gain = gain_sum.reshape(pair_count * width)
    else:
        gain_table = lax.dynamic_update_slice_in_dim(
            jnp.zeros((HEADS, width), jnp.float32), gain_sum.reshape(pair_count, width), head_first, 0
        ).reshape(HEADS * width)
        everything = lax.psum(gain_table, ("ctx", "dp"))
        share = gain.shape[0]
        grad_gain = lax.dynamic_slice_in_dim(everything, lax.axis_index("dp") * share, share, 0)
    return (grad_queries, grad_keys, grad_values, grad_gain)


def solution(mesh):
    rows = P("dp", "ctx", None)
    return jax.shard_map(
        on_device,
        mesh=mesh,
        in_specs=(rows, rows, rows, rows, P("dp"), P(), P()),
        out_specs=(rows, rows, rows, P("dp")),
        check_vma=False,
    )
```

```python
import functools
import math

import jax
import jax.numpy as jnp
from jax import lax
from jax.experimental import pallas as pl
from jax.experimental.pallas import tpu as pltpu
from jax.sharding import PartitionSpec as P

HEADS = 8
BLK = 128
WBLK = 8
PREV = (WBLK - 1) * BLK
GROUP = 2 * BLK
LOG2E = 1.4426950408889634
NEG = -1e30
M_ROW, L_ROW, D_ROW = 0, 1, 2
LIGHT, HEAVY = 1, 10**10
FEWEST = 4
LONG = 5
RIDERS = 16


def shift(value, axis, by):
    length = lax.axis_size(axis)
    pairs = [(i, (i + by) % length) for i in range(length)]
    return lax.ppermute(value, axis, pairs)


def mm(left, right):
    return lax.dot_general(left, right, (((1,), (0,)), ((), ())), preferred_element_type=jnp.float32)


def mm_t(left, right):
    return lax.dot_general(left, right, (((1,), (1,)), ((), ())), preferred_element_type=jnp.float32)


def groups(rows):
    return [(start, min(start + GROUP, rows)) for start in range(0, rows, GROUP)]


def halo_chunks(halo, rows):
    ahead = PREV - halo
    return [
        (max(0, start - ahead), min(halo, stop - ahead), min(stop, PREV))
        for start, stop in groups(rows)
        if start < PREV and stop > ahead
    ]


def halo_from(start, halo):
    return max(0, start - (PREV - halo))


def load_kernel(
    doc_hbm, win_hbm, k_hbm, v_hbm, q_hbm, g_hbm,
    k_ref, v_ref, q_ref, g_ref, low_ref, size_ref, doc_ref, win_ref, sems,
):
    pair = pl.program_id(0)
    moves = [(doc_hbm, doc_ref), (win_hbm, win_ref)]
    moves += [
        (source.at[pair], target.at[0])
        for source, target in ((k_hbm, k_ref), (v_hbm, v_ref), (q_hbm, q_ref), (g_hbm, g_ref))
    ]
    copies = [pltpu.make_async_copy(source, target, sems.at[i]) for i, (source, target) in enumerate(moves)]
    for copy in copies:
        copy.start()
    rows = q_ref.shape[1]
    copies[0].wait()
    copies[1].wait()
    reach = jnp.zeros((), jnp.int32)
    for first in range(0, doc_ref.shape[1], rows):
        reach = jnp.maximum(
            reach, first - jnp.min(jnp.maximum(doc_ref[:, first : first + rows], win_ref[:, first : first + rows]))
        )
    size_ref[0] = jnp.clip((reach + BLK - 1) // BLK, FEWEST, WBLK - 1) - FEWEST
    first_row = pl.multiple_of(lax.axis_index("ctx") * rows, BLK)
    seq_index = lax.axis_index("dp") * pl.num_programs(0) // HEADS
    own = (pl.ds(seq_index, 1), pl.ds(first_row, rows))
    low_ref[...] = jnp.maximum(doc_ref[own], win_ref[own]) - first_row
    for copy in copies[2:]:
        copy.wait()


def own_stats_kernel(
    q_ref, k_ref, v_ref, g_ref, gain_ref, low_ref,
    scaled_ref, keyt_ref, stats_ref, weight_ref, slope_ref, *, factor, step,
):
    rows = q_ref.shape[1]
    keyt_ref[0] = k_ref[0].T
    scaled_ref[0] = (q_ref[0].astype(jnp.float32) * gain_ref[0]).astype(jnp.bfloat16)

    @pl.loop(0, rows // step)
    def _(group):
        own = pl.ds(pl.multiple_of(group * step, step), step)
        logits = mm_t(k_ref[0], scaled_ref[0, own, :]) * factor
        key_at = lax.broadcasted_iota(jnp.int32, logits.shape, 0)
        query_at = group * step + lax.broadcasted_iota(jnp.int32, (1, step), 1)
        visible = (key_at >= low_ref[:, own]) & (key_at <= query_at)
        logits = jnp.where(visible, logits, NEG)
        top = jnp.max(logits, axis=0, keepdims=True)
        weights = jnp.exp2(logits - top)
        slopes = mm_t(v_ref[0], g_ref[0, own, :])
        weight_ref[0, :, own] = weights
        slope_ref[0, :, own] = slopes
        stats_ref[0, M_ROW : M_ROW + 1, own] = top
        stats_ref[0, L_ROW : L_ROW + 1, own] = jnp.sum(weights, axis=0, keepdims=True)
        stats_ref[0, D_ROW : D_ROW + 1, own] = jnp.sum(weights * slopes, axis=0, keepdims=True)


def probs_kernel(
    scaled_ref, g_ref, low_ref, part_ref, kh_ref, delta_ref, share_ref, hprobs_ref, dv_ref, *, factor
):
    rows = scaled_ref.shape[1]
    halo = kh_ref.shape[1]
    for start, stop in groups(rows):
        own_top = part_ref[0, M_ROW : M_ROW + 1, start:stop]
        total = part_ref[0, L_ROW : L_ROW + 1, start:stop]
        if start < PREV:
            first = halo_from(start, halo)
            logits = mm_t(kh_ref[0, first:, :], scaled_ref[0, start:stop, :]) * factor
            key_at = (first - halo) + lax.broadcasted_iota(jnp.int32, logits.shape, 0)
            query_block = start + lax.broadcasted_iota(jnp.int32, (1, stop - start), 1) & -BLK
            lowest = jnp.maximum(low_ref[:, start:stop], query_block - PREV)
            logits = jnp.where(key_at >= lowest, logits, NEG)
            top = jnp.maximum(own_top, jnp.max(logits, axis=0, keepdims=True))
            weights = jnp.exp2(logits - top)
            shrink = jnp.exp2(own_top - top)
            total = total * shrink + jnp.sum(weights, axis=0, keepdims=True)
            inverse = 1.0 / total
            hprobs_ref[0, first:, start:stop] = (weights * inverse).astype(jnp.bfloat16)
            share = shrink * inverse
        else:
            share = 1.0 / total
        delta_ref[0, 0:1, start:stop] = part_ref[0, D_ROW : D_ROW + 1, start:stop] * share
        share_ref[0, 0:1, start:stop] = share
    for first, last, seen in halo_chunks(halo, rows):
        dv_ref[0, first:last, :] = mm(hprobs_ref[0, first:last, :seen], g_ref[0, :seen, :]).astype(jnp.bfloat16)


def riders_of(terms):
    riders = []
    for _ in range(3):
        riders.append(terms.astype(jnp.bfloat16))
        terms = terms - riders[-1].astype(jnp.float32)
    filler = jnp.zeros((RIDERS - 3, terms.shape[1]), jnp.bfloat16)
    return jnp.concatenate(riders + [filler], axis=0)


def grads_kernel(
    q_ref, scaled_ref, g_ref, keyt_ref, part_ref, share_ref, hprobs_ref, weight_ref, slope_ref, kh_ref, vh_ref,
    dq_ref, dk_ref, head_ref, grads_ref, hgrads_ref, *, score_scale,
):
    rows = q_ref.shape[1]
    halo = kh_ref.shape[1]
    halo_cols = kh_ref[0].T
    head_sum = jnp.zeros((1, q_ref.shape[2]), jnp.float32)
    spans = groups(rows)
    deltas, halo_slopes = [], []
    for start, stop in spans:
        delta = part_ref[0, 0:1, start:stop]
        slopes = None
        if start < PREV:
            first = halo_from(start, halo)
            slopes = mm_t(vh_ref[0, first:, :], g_ref[0, start:stop, :])
            delta = delta + jnp.sum(hprobs_ref[0, first:, start:stop].astype(jnp.float32) * slopes, axis=0, keepdims=True)
        deltas.append(delta)
        halo_slopes.append(slopes)
    for (start, stop), delta, slopes in zip(spans, deltas, halo_slopes):
        if slopes is not None:
            first = halo_from(start, halo)
            hgrads_ref[first:, start:stop] = (
                hprobs_ref[0, first:, start:stop].astype(jnp.float32) * (slopes - delta)
            ).astype(jnp.bfloat16)
        probs = (weight_ref[0, :stop, start:stop] * share_ref[0, 0:1, start:stop]).astype(jnp.bfloat16).astype(jnp.float32)
        grads_ref[0, :stop, start:stop] = (probs * (slope_ref[0, :stop, start:stop] - delta)).astype(jnp.bfloat16)
        if stop < rows:
            grads_ref[0, stop:, start:stop] = jnp.zeros((rows - stop, stop - start), jnp.bfloat16)
    for start, stop in spans:
        dq = mm(keyt_ref[0, :, :stop], grads_ref[0, :stop, start:stop])
        if start < PREV:
            first = halo_from(start, halo)
            dq = dq + mm(halo_cols[:, first:], hgrads_ref[first:, start:stop])
        dq = dq.T * score_scale
        dq_ref[0, start:stop, :] = dq
        head_sum = head_sum + jnp.sum(dq * q_ref[0, start:stop, :].astype(jnp.float32), axis=0, keepdims=True)
    head_ref[0] = head_sum
    dk_ref[0, halo:, :] = riders_of(head_sum)
    for first, last, seen in halo_chunks(halo, rows):
        dk_ref[0, first:last, :] = (mm(hgrads_ref[first:last, :seen], scaled_ref[0, :seen, :]) * score_scale).astype(
            jnp.bfloat16
        )


def own_keys_kernel(
    g_ref, scaled_ref, weight_ref, share_ref, grads_ref, dq_ref, gain_ref, back_ref, gq_ref, dv_ref, dk_ref, dsum_ref, *, score_scale, step
):
    rows = g_ref.shape[1]
    gq_ref[0] = (dq_ref[0] * gain_ref[0]).astype(jnp.bfloat16)
    lead = rows - back_ref.shape[1]

    @pl.loop(0, rows // step)
    def _(group):
        own = pl.ds(pl.multiple_of(group * step, step), step)
        probs = (weight_ref[0, own, :] * share_ref[0, 0:1, :]).astype(jnp.bfloat16)
        dsum_ref[own, :] = mm(probs, g_ref[0])
        dk_ref[0, own, :] = mm(grads_ref[0, own, :], scaled_ref[0]) * score_scale

    if lead:
        dv_ref[0, :lead, :] = dsum_ref[:lead, :].astype(jnp.bfloat16)
    dv_ref[0, lead:, :] = (dsum_ref[lead:, :] + back_ref[0].astype(jnp.float32)).astype(jnp.bfloat16)


def finish_kernel(own_ref, back_ref, *refs, riding):
    terms, (dk_ref, gain_ref) = refs[:-2], refs[-2:]
    halo = back_ref.shape[1] - RIDERS
    lead = own_ref.shape[1] - halo
    if lead:
        dk_ref[0, :lead, :] = own_ref[0, :lead, :].astype(jnp.bfloat16)
    dk_ref[0, lead:, :] = (own_ref[0, lead:, :] + back_ref[0, :halo, :].astype(jnp.float32)).astype(jnp.bfloat16)
    total = terms[0][0]
    for term in terms[1:]:
        total = total + term[0]
    if riding:
        total = total + jnp.sum(back_ref[0, halo:, :].astype(jnp.float32), axis=0, keepdims=True)
    gain_ref[0] = total


def whole(shape):
    return pl.BlockSpec((1,) + shape, lambda p: (p,) + (0,) * len(shape))


def call(kernel, pair_count, in_specs, outs, weight, scratch=(), **fixed):
    specs, shapes = zip(*outs)
    return pl.pallas_call(
        functools.partial(kernel, **fixed),
        grid=(pair_count,),
        in_specs=in_specs,
        out_specs=specs,
        out_shape=shapes,
        scratch_shapes=list(scratch),
        compiler_params=pltpu.CompilerParams(vmem_limit_bytes=32 * 1024 * 1024),
        cost_estimate=pl.CostEstimate(flops=weight, bytes_accessed=1, transcendentals=0),
    )


def band(halo, aligned, keys_in, values_in, queries_in, grad_in, lower, gain_rows):
    pair_count, rows, width = queries_in.shape
    score_scale = 1.0 / math.sqrt(width)
    factor = score_scale * LOG2E
    bf16, f32 = jnp.bfloat16, jnp.float32
    key_halo = shift(keys_in[:, rows - halo :], "ctx", 1)
    value_halo = shift(values_in[:, rows - halo :], "ctx", 1)

    row_spec = whole((rows, width))
    gain_spec = whole((1, width))
    stat_spec = whole((8, rows))
    delta_spec = whole((1, rows))
    halo_spec = whole((halo, width))
    ridden_spec = whole((halo + RIDERS, width))
    keyt_spec = whole((width, rows))
    own_sq = whole((rows, rows))
    halo_sq = whole((halo, rows))
    low_spec = pl.BlockSpec((1, rows), lambda p: (0, 0))

    def shaped(shape, dtype):
        return jax.ShapeDtypeStruct((pair_count,) + shape, dtype)

    row_out = (row_spec, shaped((rows, width), bf16))
    wide_out = (row_spec, shaped((rows, width), f32))
    scaled, key_cols, part, own_weights, own_slopes = call(
        own_stats_kernel,
        pair_count,
        [row_spec] * 4 + [gain_spec, low_spec],
        (
            row_out,
            (keyt_spec, shaped((width, rows), bf16)),
            (stat_spec, shaped((8, rows), f32)),
            (own_sq, shaped((rows, rows), f32)),
            (own_sq, shaped((rows, rows), f32)),
        ),
        LIGHT,
        factor=factor,
        step=BLK if halo >= LONG * BLK else GROUP,
    )(queries_in, keys_in, values_in, grad_in, gain_rows, lower)

    own_delta, own_share, halo_probs, dv_halo = call(
        probs_kernel,
        pair_count,
        [row_spec, row_spec, low_spec, stat_spec, halo_spec],
        (
            (delta_spec, shaped((1, rows), f32)),
            (delta_spec, shaped((1, rows), f32)),
            (halo_sq, shaped((halo, rows), bf16)),
            (halo_spec, shaped((halo, width), bf16)),
        ),
        LIGHT,
        factor=factor,
    )(scaled, grad_in, lower, part, key_halo)
    dv_back = shift(dv_halo, "ctx", -1)

    dq, dk_halo, head_terms, own_grads = call(
        grads_kernel,
        pair_count,
        [row_spec] * 3 + [keyt_spec, delta_spec, delta_spec, halo_sq, own_sq, own_sq, halo_spec, halo_spec],
        (
            wide_out,
            (ridden_spec, shaped((halo + RIDERS, width), bf16)),
            (gain_spec, shaped((1, width), f32)),
            (own_sq, shaped((rows, rows), bf16)),
        ),
        HEAVY,
        scratch=[pltpu.VMEM((halo, rows), bf16)],
        score_scale=score_scale,
    )(
        queries_in, scaled, grad_in, key_cols, own_delta, own_share, halo_probs, own_weights, own_slopes,
        key_halo, value_halo,
    )
    dk_back = shift(dk_halo, "ctx", -1)
    length = lax.axis_size("ctx")
    riding = aligned and 1 < length <= 4
    terms = [head_terms]
    if riding:
        terms += [shift(head_terms, "ctx", by) for by in reversed(range(1, length - 1))]
    elif aligned:
        terms = [lax.psum(head_terms, "ctx")]

    grad_queries, grad_values, dk_own = call(
        own_keys_kernel,
        pair_count,
        [row_spec, row_spec, own_sq, delta_spec, own_sq, row_spec, gain_spec, halo_spec],
        (row_out, row_out, wide_out),
        10**9,
        scratch=[pltpu.VMEM((rows, width), f32)],
        score_scale=score_scale,
        step=BLK if halo >= LONG * BLK else GROUP,
    )(grad_in, scaled, own_weights, own_share, own_grads, dq, gain_rows, dv_back)
    grad_keys, gain_sum = call(
        finish_kernel,
        pair_count,
        [row_spec, ridden_spec] + [gain_spec] * len(terms),
        (row_out, (gain_spec, shaped((1, width), f32))),
        LIGHT,
        riding=riding,
    )(dk_own, dk_back, *terms)
    return grad_queries, grad_keys, grad_values, gain_sum


def on_device(queries, keys, values, grad_out, gain, doc_start, win_start):
    pair_count, rows, width = queries.shape
    head_first = lax.axis_index("dp") * pair_count % HEADS
    aligned = lax.axis_size("dp") * pair_count == HEADS and gain.shape[0] == pair_count * width
    if aligned:
        gain_rows = gain.reshape(pair_count, 1, width)
    else:
        full_gain = lax.all_gather(gain, "dp", axis=0, tiled=True)
        gain_rows = lax.dynamic_slice_in_dim(
            full_gain.reshape(HEADS, width), head_first, pair_count, 0
        ).reshape(pair_count, 1, width)

    hbm = pl.BlockSpec(memory_space=pltpu.HBM)
    row_out = (whole((rows, width)), jax.ShapeDtypeStruct((pair_count, rows, width), jnp.bfloat16))
    *loaded, size = call(
        load_kernel,
        pair_count,
        [hbm] * 6,
        [row_out] * 4
        + [
            (pl.BlockSpec((1, rows), lambda p: (0, 0)), jax.ShapeDtypeStruct((1, rows), jnp.int32)),
            (pl.BlockSpec(memory_space=pltpu.SMEM), jax.ShapeDtypeStruct((1,), jnp.int32)),
        ],
        LIGHT,
        scratch=[pltpu.VMEM(doc_start.shape, jnp.int32)] * 2 + [pltpu.SemaphoreType.DMA((6,))],
    )(*(pltpu.with_memory_space_constraint(x, pltpu.HBM) for x in (doc_start, win_start, keys, values, queries, grad_out)))
    grad_queries, grad_keys, grad_values, gain_sum = lax.switch(
        size[0],
        [functools.partial(band, blocks * BLK, aligned) for blocks in range(FEWEST, WBLK)],
        *loaded, gain_rows,
    )
    if aligned:
        grad_gain = gain_sum.reshape(pair_count * width)
    else:
        gain_table = lax.dynamic_update_slice_in_dim(
            jnp.zeros((HEADS, width), jnp.float32), gain_sum.reshape(pair_count, width), head_first, 0
        ).reshape(HEADS * width)
        everything = lax.psum(gain_table, ("ctx", "dp"))
        share = gain.shape[0]
        grad_gain = lax.dynamic_slice_in_dim(everything, lax.axis_index("dp") * share, share, 0)
    return (grad_queries, grad_keys, grad_values, grad_gain)


def solution(mesh):
    rows = P("dp", "ctx", None)
    return jax.shard_map(
        on_device,
        mesh=mesh,
        in_specs=(rows, rows, rows, rows, P("dp"), P(), P()),
        out_specs=(rows, rows, rows, P("dp")),
        check_vma=False,
    )
```

```python
import functools
import math

import jax
import jax.numpy as jnp
from jax import lax
from jax.experimental import pallas as pl
from jax.experimental.pallas import tpu as pltpu
from jax.sharding import PartitionSpec as P

HEADS = 8
BLK = 128
WBLK = 8
PREV = (WBLK - 1) * BLK
GROUP = 2 * BLK
LOG2E = 1.4426950408889634
NEG = -1e30
M_ROW, L_ROW, D_ROW = 0, 1, 2
LIGHT, HEAVY = 1, 10**10
FEWEST = 4
LONG = 5
RIDERS = 16


def shift(value, axis, by):
    length = lax.axis_size(axis)
    pairs = [(i, (i + by) % length) for i in range(length)]
    return lax.ppermute(value, axis, pairs)


def mm(left, right):
    return lax.dot_general(left, right, (((1,), (0,)), ((), ())), preferred_element_type=jnp.float32)


def mm_t(left, right):
    return lax.dot_general(left, right, (((1,), (1,)), ((), ())), preferred_element_type=jnp.float32)


def groups(rows):
    return [(start, min(start + GROUP, rows)) for start in range(0, rows, GROUP)]


def query_spans(rows):
    cut = min(PREV, rows)
    return groups(cut) + [(cut + start, cut + stop) for start, stop in groups(rows - cut)]


def halo_chunks(halo, rows):
    ahead = PREV - halo
    return [
        (max(0, start - ahead), min(halo, stop - ahead), min(stop, PREV))
        for start, stop in groups(rows)
        if start < PREV and stop > ahead
    ]


def halo_from(start, halo):
    return max(0, start - (PREV - halo))


def load_kernel(
    doc_hbm, win_hbm, k_hbm, v_hbm, q_hbm, g_hbm,
    k_ref, v_ref, q_ref, g_ref, low_ref, size_ref, doc_ref, win_ref, sems,
):
    pair = pl.program_id(0)
    moves = [(doc_hbm, doc_ref), (win_hbm, win_ref)]
    moves += [
        (source.at[pair], target.at[0])
        for source, target in ((k_hbm, k_ref), (v_hbm, v_ref), (q_hbm, q_ref), (g_hbm, g_ref))
    ]
    copies = [pltpu.make_async_copy(source, target, sems.at[i]) for i, (source, target) in enumerate(moves)]
    for copy in copies:
        copy.start()
    rows = q_ref.shape[1]
    copies[0].wait()
    copies[1].wait()
    reach = jnp.zeros((), jnp.int32)
    for first in range(0, doc_ref.shape[1], rows):
        reach = jnp.maximum(
            reach, first - jnp.min(jnp.maximum(doc_ref[:, first : first + rows], win_ref[:, first : first + rows]))
        )
    size_ref[0] = jnp.clip((reach + BLK - 1) // BLK, FEWEST, WBLK - 1) - FEWEST
    first_row = pl.multiple_of(lax.axis_index("ctx") * rows, BLK)
    seq_index = lax.axis_index("dp") * pl.num_programs(0) // HEADS
    own = (pl.ds(seq_index, 1), pl.ds(first_row, rows))
    low_ref[...] = jnp.maximum(doc_ref[own], win_ref[own]) - first_row
    for copy in copies[2:]:
        copy.wait()


def own_stats_kernel(
    q_ref, k_ref, v_ref, g_ref, gain_ref, low_ref,
    scaled_ref, keyt_ref, stats_ref, weight_ref, slope_ref, *, factor, step,
):
    rows = q_ref.shape[1]
    keyt_ref[0] = k_ref[0].T
    scaled_ref[0] = (q_ref[0].astype(jnp.float32) * gain_ref[0]).astype(jnp.bfloat16)

    @pl.loop(0, rows // step)
    def _(group):
        own = pl.ds(pl.multiple_of(group * step, step), step)
        logits = mm_t(k_ref[0], scaled_ref[0, own, :]) * factor
        key_at = lax.broadcasted_iota(jnp.int32, logits.shape, 0)
        query_at = group * step + lax.broadcasted_iota(jnp.int32, (1, step), 1)
        visible = (key_at >= low_ref[:, own]) & (key_at <= query_at)
        logits = jnp.where(visible, logits, NEG)
        top = jnp.max(logits, axis=0, keepdims=True)
        weights = jnp.exp2(logits - top)
        slopes = mm_t(v_ref[0], g_ref[0, own, :])
        weight_ref[0, :, own] = weights
        slope_ref[0, :, own] = slopes
        stats_ref[0, M_ROW : M_ROW + 1, own] = top
        stats_ref[0, L_ROW : L_ROW + 1, own] = jnp.sum(weights, axis=0, keepdims=True)
        stats_ref[0, D_ROW : D_ROW + 1, own] = jnp.sum(weights * slopes, axis=0, keepdims=True)


def probs_kernel(
    scaled_ref, g_ref, low_ref, part_ref, kh_ref, delta_ref, share_ref, hprobs_ref, dv_ref, *, factor
):
    rows = scaled_ref.shape[1]
    halo = kh_ref.shape[1]
    for start, stop in query_spans(rows):
        own_top = part_ref[0, M_ROW : M_ROW + 1, start:stop]
        total = part_ref[0, L_ROW : L_ROW + 1, start:stop]
        if start < PREV:
            first = halo_from(start, halo)
            logits = mm_t(kh_ref[0, first:, :], scaled_ref[0, start:stop, :]) * factor
            key_at = (first - halo) + lax.broadcasted_iota(jnp.int32, logits.shape, 0)
            query_block = start + lax.broadcasted_iota(jnp.int32, (1, stop - start), 1) & -BLK
            lowest = jnp.maximum(low_ref[:, start:stop], query_block - PREV)
            logits = jnp.where(key_at >= lowest, logits, NEG)
            top = jnp.maximum(own_top, jnp.max(logits, axis=0, keepdims=True))
            weights = jnp.exp2(logits - top)
            shrink = jnp.exp2(own_top - top)
            total = total * shrink + jnp.sum(weights, axis=0, keepdims=True)
            inverse = 1.0 / total
            hprobs_ref[0, first:, start:stop] = (weights * inverse).astype(jnp.bfloat16)
            share = shrink * inverse
        else:
            share = 1.0 / total
            first = halo_from(start // GROUP * GROUP, halo)
            hprobs_ref[0, first:, start:stop] = jnp.zeros((halo - first, stop - start), jnp.bfloat16)
        delta_ref[0, 0:1, start:stop] = part_ref[0, D_ROW : D_ROW + 1, start:stop] * share
        share_ref[0, 0:1, start:stop] = share
    for first, last, seen in halo_chunks(halo, rows):
        dv_ref[0, first:last, :] = mm(hprobs_ref[0, first:last, :seen], g_ref[0, :seen, :]).astype(jnp.bfloat16)


def riders_of(terms):
    riders = []
    for _ in range(3):
        riders.append(terms.astype(jnp.bfloat16))
        terms = terms - riders[-1].astype(jnp.float32)
    filler = jnp.zeros((RIDERS - 3, terms.shape[1]), jnp.bfloat16)
    return jnp.concatenate(riders + [filler], axis=0)


def grads_kernel(
    q_ref, scaled_ref, g_ref, keyt_ref, part_ref, share_ref, hprobs_ref, weight_ref, slope_ref, kh_ref, vh_ref,
    dq_ref, dk_ref, head_ref, grads_ref, hgrads_ref, *, score_scale,
):
    rows = q_ref.shape[1]
    halo = kh_ref.shape[1]
    halo_cols = kh_ref[0].T
    head_sum = jnp.zeros((1, q_ref.shape[2]), jnp.float32)
    spans = groups(rows)
    deltas, halo_slopes = [], []
    for start, stop in spans:
        delta = part_ref[0, 0:1, start:stop]
        slopes = None
        if start < PREV:
            first = halo_from(start, halo)
            slopes = mm_t(vh_ref[0, first:, :], g_ref[0, start:stop, :])
            delta = delta + jnp.sum(hprobs_ref[0, first:, start:stop].astype(jnp.float32) * slopes, axis=0, keepdims=True)
        deltas.append(delta)
        halo_slopes.append(slopes)
    for (start, stop), delta, slopes in zip(spans, deltas, halo_slopes):
        if slopes is not None:
            first = halo_from(start, halo)
            hgrads_ref[first:, start:stop] = (
                hprobs_ref[0, first:, start:stop].astype(jnp.float32) * (slopes - delta)
            ).astype(jnp.bfloat16)
        probs = (weight_ref[0, :stop, start:stop] * share_ref[0, 0:1, start:stop]).astype(jnp.bfloat16).astype(jnp.float32)
        grads_ref[0, :stop, start:stop] = (probs * (slope_ref[0, :stop, start:stop] - delta)).astype(jnp.bfloat16)
        if stop < rows:
            grads_ref[0, stop:, start:stop] = jnp.zeros((rows - stop, stop - start), jnp.bfloat16)
    for start, stop in spans:
        dq = mm(keyt_ref[0, :, :stop], grads_ref[0, :stop, start:stop])
        if start < PREV:
            first = halo_from(start, halo)
            dq = dq + mm(halo_cols[:, first:], hgrads_ref[first:, start:stop])
        dq = dq.T * score_scale
        dq_ref[0, start:stop, :] = dq
        head_sum = head_sum + jnp.sum(dq * q_ref[0, start:stop, :].astype(jnp.float32), axis=0, keepdims=True)
    head_ref[0] = head_sum
    dk_ref[0, halo:, :] = riders_of(head_sum)
    for first, last, seen in halo_chunks(halo, rows):
        dk_ref[0, first:last, :] = (mm(hgrads_ref[first:last, :seen], scaled_ref[0, :seen, :]) * score_scale).astype(
            jnp.bfloat16
        )


def own_keys_kernel(
    g_ref, scaled_ref, weight_ref, share_ref, grads_ref, dq_ref, gain_ref, back_ref, gq_ref, dv_ref, dk_ref, dsum_ref, *, score_scale, step
):
    rows = g_ref.shape[1]
    lead = rows - back_ref.shape[1]

    @pl.loop(0, rows // step)
    def _(group):
        own = pl.ds(pl.multiple_of(group * step, step), step)
        probs = (weight_ref[0, own, :] * share_ref[0, 0:1, :]).astype(jnp.bfloat16)
        dsum_ref[own, :] = mm(probs, g_ref[0])
        dk_ref[0, own, :] = mm(grads_ref[0, own, :], scaled_ref[0]) * score_scale
        gq_ref[0, own, :] = (dq_ref[0, own, :] * gain_ref[0]).astype(jnp.bfloat16)

    if lead:
        dv_ref[0, :lead, :] = dsum_ref[:lead, :].astype(jnp.bfloat16)
    dv_ref[0, lead:, :] = (dsum_ref[lead:, :] + back_ref[0].astype(jnp.float32)).astype(jnp.bfloat16)


def finish_kernel(own_ref, back_ref, *refs, riding):
    terms, (dk_ref, gain_ref) = refs[:-2], refs[-2:]
    halo = back_ref.shape[1] - RIDERS
    lead = own_ref.shape[1] - halo
    if lead:
        dk_ref[0, :lead, :] = own_ref[0, :lead, :].astype(jnp.bfloat16)
    dk_ref[0, lead:, :] = (own_ref[0, lead:, :] + back_ref[0, :halo, :].astype(jnp.float32)).astype(jnp.bfloat16)
    total = terms[0][0]
    for term in terms[1:]:
        total = total + term[0]
    if riding:
        total = total + jnp.sum(back_ref[0, halo:, :].astype(jnp.float32), axis=0, keepdims=True)
    gain_ref[0] = total


def whole(shape):
    return pl.BlockSpec((1,) + shape, lambda p: (p,) + (0,) * len(shape))


def call(kernel, pair_count, in_specs, outs, weight, scratch=(), **fixed):
    specs, shapes = zip(*outs)
    return pl.pallas_call(
        functools.partial(kernel, **fixed),
        grid=(pair_count,),
        in_specs=in_specs,
        out_specs=specs,
        out_shape=shapes,
        scratch_shapes=list(scratch),
        compiler_params=pltpu.CompilerParams(vmem_limit_bytes=32 * 1024 * 1024),
        cost_estimate=pl.CostEstimate(flops=weight, bytes_accessed=1, transcendentals=0),
    )


def band(halo, aligned, keys_in, values_in, queries_in, grad_in, lower, gain_rows):
    pair_count, rows, width = queries_in.shape
    score_scale = 1.0 / math.sqrt(width)
    factor = score_scale * LOG2E
    bf16, f32 = jnp.bfloat16, jnp.float32
    key_halo = shift(keys_in[:, rows - halo :], "ctx", 1)
    value_halo = shift(values_in[:, rows - halo :], "ctx", 1)

    row_spec = whole((rows, width))
    gain_spec = whole((1, width))
    stat_spec = whole((8, rows))
    delta_spec = whole((1, rows))
    halo_spec = whole((halo, width))
    ridden_spec = whole((halo + RIDERS, width))
    keyt_spec = whole((width, rows))
    own_sq = whole((rows, rows))
    halo_sq = whole((halo, rows))
    low_spec = pl.BlockSpec((1, rows), lambda p: (0, 0))

    def shaped(shape, dtype):
        return jax.ShapeDtypeStruct((pair_count,) + shape, dtype)

    row_out = (row_spec, shaped((rows, width), bf16))
    wide_out = (row_spec, shaped((rows, width), f32))
    scaled, key_cols, part, own_weights, own_slopes = call(
        own_stats_kernel,
        pair_count,
        [row_spec] * 4 + [gain_spec, low_spec],
        (
            row_out,
            (keyt_spec, shaped((width, rows), bf16)),
            (stat_spec, shaped((8, rows), f32)),
            (own_sq, shaped((rows, rows), f32)),
            (own_sq, shaped((rows, rows), f32)),
        ),
        LIGHT,
        factor=factor,
        step=BLK if halo >= LONG * BLK else GROUP,
    )(queries_in, keys_in, values_in, grad_in, gain_rows, lower)

    own_delta, own_share, halo_probs, dv_halo = call(
        probs_kernel,
        pair_count,
        [row_spec, row_spec, low_spec, stat_spec, halo_spec],
        (
            (delta_spec, shaped((1, rows), f32)),
            (delta_spec, shaped((1, rows), f32)),
            (halo_sq, shaped((halo, rows), bf16)),
            (halo_spec, shaped((halo, width), bf16)),
        ),
        LIGHT,
        factor=factor,
    )(scaled, grad_in, lower, part, key_halo)
    dv_back = shift(dv_halo, "ctx", -1)

    dq, dk_halo, head_terms, own_grads = call(
        grads_kernel,
        pair_count,
        [row_spec] * 3 + [keyt_spec, delta_spec, delta_spec, halo_sq, own_sq, own_sq, halo_spec, halo_spec],
        (
            wide_out,
            (ridden_spec, shaped((halo + RIDERS, width), bf16)),
            (gain_spec, shaped((1, width), f32)),
            (own_sq, shaped((rows, rows), bf16)),
        ),
        HEAVY,
        scratch=[pltpu.VMEM((halo, rows), bf16)],
        score_scale=score_scale,
    )(
        queries_in, scaled, grad_in, key_cols, own_delta, own_share, halo_probs, own_weights, own_slopes,
        key_halo, value_halo,
    )
    dk_back = shift(dk_halo, "ctx", -1)
    length = lax.axis_size("ctx")
    riding = aligned and 1 < length <= 4
    terms = [head_terms]
    if riding:
        terms += [shift(head_terms, "ctx", by) for by in reversed(range(1, length - 1))]
    elif aligned:
        terms = [lax.psum(head_terms, "ctx")]

    grad_queries, grad_values, dk_own = call(
        own_keys_kernel,
        pair_count,
        [row_spec, row_spec, own_sq, delta_spec, own_sq, row_spec, gain_spec, halo_spec],
        (row_out, row_out, wide_out),
        10**9,
        scratch=[pltpu.VMEM((rows, width), f32)],
        score_scale=score_scale,
        step=BLK if halo >= LONG * BLK else GROUP,
    )(grad_in, scaled, own_weights, own_share, own_grads, dq, gain_rows, dv_back)
    grad_keys, gain_sum = call(
        finish_kernel,
        pair_count,
        [row_spec, ridden_spec] + [gain_spec] * len(terms),
        (row_out, (gain_spec, shaped((1, width), f32))),
        LIGHT,
        riding=riding,
    )(dk_own, dk_back, *terms)
    return grad_queries, grad_keys, grad_values, gain_sum


def on_device(queries, keys, values, grad_out, gain, doc_start, win_start):
    pair_count, rows, width = queries.shape
    head_first = lax.axis_index("dp") * pair_count % HEADS
    aligned = lax.axis_size("dp") * pair_count == HEADS and gain.shape[0] == pair_count * width
    if aligned:
        gain_rows = gain.reshape(pair_count, 1, width)
    else:
        full_gain = lax.all_gather(gain, "dp", axis=0, tiled=True)
        gain_rows = lax.dynamic_slice_in_dim(
            full_gain.reshape(HEADS, width), head_first, pair_count, 0
        ).reshape(pair_count, 1, width)

    hbm = pl.BlockSpec(memory_space=pltpu.HBM)
    row_out = (whole((rows, width)), jax.ShapeDtypeStruct((pair_count, rows, width), jnp.bfloat16))
    *loaded, size = call(
        load_kernel,
        pair_count,
        [hbm] * 6,
        [row_out] * 4
        + [
            (pl.BlockSpec((1, rows), lambda p: (0, 0)), jax.ShapeDtypeStruct((1, rows), jnp.int32)),
            (pl.BlockSpec(memory_space=pltpu.SMEM), jax.ShapeDtypeStruct((1,), jnp.int32)),
        ],
        LIGHT,
        scratch=[pltpu.VMEM(doc_start.shape, jnp.int32)] * 2 + [pltpu.SemaphoreType.DMA((6,))],
    )(*(pltpu.with_memory_space_constraint(x, pltpu.HBM) for x in (doc_start, win_start, keys, values, queries, grad_out)))
    grad_queries, grad_keys, grad_values, gain_sum = lax.switch(
        size[0],
        [functools.partial(band, blocks * BLK, aligned) for blocks in range(FEWEST, WBLK)],
        *loaded, gain_rows,
    )
    if aligned:
        grad_gain = gain_sum.reshape(pair_count * width)
    else:
        gain_table = lax.dynamic_update_slice_in_dim(
            jnp.zeros((HEADS, width), jnp.float32), gain_sum.reshape(pair_count, width), head_first, 0
        ).reshape(HEADS * width)
        everything = lax.psum(gain_table, ("ctx", "dp"))
        share = gain.shape[0]
        grad_gain = lax.dynamic_slice_in_dim(everything, lax.axis_index("dp") * share, share, 0)
    return (grad_queries, grad_keys, grad_values, grad_gain)


def solution(mesh):
    rows = P("dp", "ctx", None)
    return jax.shard_map(
        on_device,
        mesh=mesh,
        in_specs=(rows, rows, rows, rows, P("dp"), P(), P()),
        out_specs=(rows, rows, rows, P("dp")),
        check_vma=False,
    )
```

```python
import functools
import math

import jax
import jax.numpy as jnp
from jax import lax
from jax.experimental import pallas as pl
from jax.experimental.pallas import tpu as pltpu
from jax.sharding import PartitionSpec as P

HEADS = 8
BLK = 128
WBLK = 8
PREV = (WBLK - 1) * BLK
GROUP = 2 * BLK
LOG2E = 1.4426950408889634
NEG = -1e30
M_ROW, L_ROW, D_ROW = 0, 1, 2
LIGHT, HEAVY = 1, 10**10
FEWEST = 4
LONG = 5
RIDERS = 16


def shift(value, axis, by):
    length = lax.axis_size(axis)
    pairs = [(i, (i + by) % length) for i in range(length)]
    return lax.ppermute(value, axis, pairs)


def mm(left, right):
    return lax.dot_general(left, right, (((1,), (0,)), ((), ())), preferred_element_type=jnp.float32)


def mm_t(left, right):
    return lax.dot_general(left, right, (((1,), (1,)), ((), ())), preferred_element_type=jnp.float32)


def groups(rows):
    return [(start, min(start + GROUP, rows)) for start in range(0, rows, GROUP)]


def halo_chunks(halo, rows):
    ahead = PREV - halo
    return [
        (max(0, start - ahead), min(halo, stop - ahead), min(stop, PREV))
        for start, stop in groups(rows)
        if start < PREV and stop > ahead
    ]


def halo_from(start, halo):
    return max(0, start - (PREV - halo))


def load_kernel(
    doc_hbm, win_hbm, k_hbm, v_hbm, q_hbm, g_hbm,
    k_ref, v_ref, q_ref, g_ref, low_ref, size_ref, doc_ref, win_ref, sems,
):
    pair = pl.program_id(0)
    moves = [(doc_hbm, doc_ref), (win_hbm, win_ref)]
    moves += [
        (source.at[pair], target.at[0])
        for source, target in ((k_hbm, k_ref), (v_hbm, v_ref), (q_hbm, q_ref), (g_hbm, g_ref))
    ]
    copies = [pltpu.make_async_copy(source, target, sems.at[i]) for i, (source, target) in enumerate(moves)]
    for copy in copies:
        copy.start()
    rows = q_ref.shape[1]
    copies[0].wait()
    copies[1].wait()
    reach = jnp.zeros((), jnp.int32)
    for first in range(0, doc_ref.shape[1], rows):
        reach = jnp.maximum(
            reach, first - jnp.min(jnp.maximum(doc_ref[:, first : first + rows], win_ref[:, first : first + rows]))
        )
    size_ref[0] = jnp.clip((reach + BLK - 1) // BLK, FEWEST, WBLK - 1) - FEWEST
    first_row = pl.multiple_of(lax.axis_index("ctx") * rows, BLK)
    seq_index = lax.axis_index("dp") * pl.num_programs(0) // HEADS
    own = (pl.ds(seq_index, 1), pl.ds(first_row, rows))
    low_ref[...] = jnp.maximum(doc_ref[own], win_ref[own]) - first_row
    for copy in copies[2:]:
        copy.wait()


def own_stats_kernel(
    q_ref, k_ref, v_ref, g_ref, gain_ref, low_ref,
    scaled_ref, keyt_ref, stats_ref, weight_ref, slope_ref, *, factor, step,
):
    rows = q_ref.shape[1]
    keyt_ref[0] = k_ref[0].T
    scaled_ref[0] = (q_ref[0].astype(jnp.float32) * gain_ref[0]).astype(jnp.bfloat16)

    @pl.loop(0, rows // step)
    def _(group):
        own = pl.ds(pl.multiple_of(group * step, step), step)
        logits = mm_t(k_ref[0], scaled_ref[0, own, :]) * factor
        key_at = lax.broadcasted_iota(jnp.int32, logits.shape, 0)
        query_at = group * step + lax.broadcasted_iota(jnp.int32, (1, step), 1)
        visible = (key_at >= low_ref[:, own]) & (key_at <= query_at)
        logits = jnp.where(visible, logits, NEG)
        top = jnp.max(logits, axis=0, keepdims=True)
        weights = jnp.exp2(logits - top)
        slopes = mm_t(v_ref[0], g_ref[0, own, :])
        weight_ref[0, :, own] = weights
        slope_ref[0, :, own] = slopes
        stats_ref[0, M_ROW : M_ROW + 1, own] = top
        stats_ref[0, L_ROW : L_ROW + 1, own] = jnp.sum(weights, axis=0, keepdims=True)
        stats_ref[0, D_ROW : D_ROW + 1, own] = jnp.sum(weights * slopes, axis=0, keepdims=True)


def probs_kernel(
    scaled_ref, g_ref, low_ref, part_ref, weight_ref, kh_ref,
    delta_ref, hprobs_ref, probs_ref, dv_ref, share_ref, *, factor, step,
):
    rows = scaled_ref.shape[1]
    halo = kh_ref.shape[1]
    for start, stop in groups(rows):
        own_top = part_ref[0, M_ROW : M_ROW + 1, start:stop]
        total = part_ref[0, L_ROW : L_ROW + 1, start:stop]
        if start < PREV:
            first = halo_from(start, halo)
            logits = mm_t(kh_ref[0, first:, :], scaled_ref[0, start:stop, :]) * factor
            key_at = (first - halo) + lax.broadcasted_iota(jnp.int32, logits.shape, 0)
            query_block = start + lax.broadcasted_iota(jnp.int32, (1, stop - start), 1) & -BLK
            lowest = jnp.maximum(low_ref[:, start:stop], query_block - PREV)
            logits = jnp.where(key_at >= lowest, logits, NEG)
            top = jnp.maximum(own_top, jnp.max(logits, axis=0, keepdims=True))
            weights = jnp.exp2(logits - top)
            shrink = jnp.exp2(own_top - top)
            total = total * shrink + jnp.sum(weights, axis=0, keepdims=True)
            inverse = 1.0 / total
            hprobs_ref[0, first:, start:stop] = (weights * inverse).astype(jnp.bfloat16)
            share = shrink * inverse
        else:
            share = 1.0 / total
        delta_ref[0, 0:1, start:stop] = part_ref[0, D_ROW : D_ROW + 1, start:stop] * share
        share_ref[:, start:stop] = share

    @pl.loop(0, rows // step)
    def _(group):
        own = pl.ds(pl.multiple_of(group * step, step), step)
        probs_ref[0, :, own] = (weight_ref[0, :, own] * share_ref[:, own]).astype(jnp.bfloat16)

    for first, last, seen in halo_chunks(halo, rows):
        dv_ref[0, first:last, :] = mm(hprobs_ref[0, first:last, :seen], g_ref[0, :seen, :]).astype(jnp.bfloat16)


def riders_of(terms):
    riders = []
    for _ in range(3):
        riders.append(terms.astype(jnp.bfloat16))
        terms = terms - riders[-1].astype(jnp.float32)
    filler = jnp.zeros((RIDERS - 3, terms.shape[1]), jnp.bfloat16)
    return jnp.concatenate(riders + [filler], axis=0)


def grads_kernel(
    q_ref, scaled_ref, g_ref, keyt_ref, part_ref, hprobs_ref, probs_ref, slope_ref, kh_ref, vh_ref,
    dq_ref, dk_ref, head_ref, grads_ref, hgrads_ref, *, score_scale,
):
    rows = q_ref.shape[1]
    halo = kh_ref.shape[1]
    halo_cols = kh_ref[0].T
    head_sum = jnp.zeros((1, q_ref.shape[2]), jnp.float32)
    spans = groups(rows)
    deltas, halo_slopes = [], []
    for start, stop in spans:
        delta = part_ref[0, 0:1, start:stop]
        slopes = None
        if start < PREV:
            first = halo_from(start, halo)
            slopes = mm_t(vh_ref[0, first:, :], g_ref[0, start:stop, :])
            delta = delta + jnp.sum(hprobs_ref[0, first:, start:stop].astype(jnp.float32) * slopes, axis=0, keepdims=True)
        deltas.append(delta)
        halo_slopes.append(slopes)
    for (start, stop), delta, slopes in zip(spans, deltas, halo_slopes):
        if slopes is not None:
            first = halo_from(start, halo)
            hgrads_ref[first:, start:stop] = (
                hprobs_ref[0, first:, start:stop].astype(jnp.float32) * (slopes - delta)
            ).astype(jnp.bfloat16)
        probs = probs_ref[0, :stop, start:stop].astype(jnp.float32)
        grads_ref[0, :stop, start:stop] = (probs * (slope_ref[0, :stop, start:stop] - delta)).astype(jnp.bfloat16)
        if stop < rows:
            grads_ref[0, stop:, start:stop] = jnp.zeros((rows - stop, stop - start), jnp.bfloat16)
    for start, stop in spans:
        dq = mm(keyt_ref[0, :, :stop], grads_ref[0, :stop, start:stop])
        if start < PREV:
            first = halo_from(start, halo)
            dq = dq + mm(halo_cols[:, first:], hgrads_ref[first:, start:stop])
        dq = dq.T * score_scale
        dq_ref[0, start:stop, :] = dq
        head_sum = head_sum + jnp.sum(dq * q_ref[0, start:stop, :].astype(jnp.float32), axis=0, keepdims=True)
    head_ref[0] = head_sum
    dk_ref[0, halo:, :] = riders_of(head_sum)
    for first, last, seen in halo_chunks(halo, rows):
        dk_ref[0, first:last, :] = (mm(hgrads_ref[first:last, :seen], scaled_ref[0, :seen, :]) * score_scale).astype(
            jnp.bfloat16
        )


def own_keys_kernel(
    g_ref, scaled_ref, probs_ref, grads_ref, dq_ref, gain_ref, back_ref, gq_ref, dv_ref, dk_ref, dsum_ref, *, score_scale, step
):
    rows = g_ref.shape[1]
    lead = rows - back_ref.shape[1]

    @pl.loop(0, rows // step)
    def _(group):
        own = pl.ds(pl.multiple_of(group * step, step), step)
        dsum_ref[own, :] = mm(probs_ref[0, own, :], g_ref[0])
        dk_ref[0, own, :] = mm(grads_ref[0, own, :], scaled_ref[0]) * score_scale
        gq_ref[0, own, :] = (dq_ref[0, own, :] * gain_ref[0]).astype(jnp.bfloat16)

    if lead:
        dv_ref[0, :lead, :] = dsum_ref[:lead, :].astype(jnp.bfloat16)
    dv_ref[0, lead:, :] = (dsum_ref[lead:, :] + back_ref[0].astype(jnp.float32)).astype(jnp.bfloat16)


def finish_kernel(own_ref, back_ref, *refs, riding):
    terms, (dk_ref, gain_ref) = refs[:-2], refs[-2:]
    halo = back_ref.shape[1] - RIDERS
    lead = own_ref.shape[1] - halo
    if lead:
        dk_ref[0, :lead, :] = own_ref[0, :lead, :].astype(jnp.bfloat16)
    dk_ref[0, lead:, :] = (own_ref[0, lead:, :] + back_ref[0, :halo, :].astype(jnp.float32)).astype(jnp.bfloat16)
    total = terms[0][0]
    for term in terms[1:]:
        total = total + term[0]
    if riding:
        total = total + jnp.sum(back_ref[0, halo:, :].astype(jnp.float32), axis=0, keepdims=True)
    gain_ref[0] = total


def whole(shape):
    return pl.BlockSpec((1,) + shape, lambda p: (p,) + (0,) * len(shape))


def call(kernel, pair_count, in_specs, outs, weight, scratch=(), **fixed):
    specs, shapes = zip(*outs)
    return pl.pallas_call(
        functools.partial(kernel, **fixed),
        grid=(pair_count,),
        in_specs=in_specs,
        out_specs=specs,
        out_shape=shapes,
        scratch_shapes=list(scratch),
        compiler_params=pltpu.CompilerParams(vmem_limit_bytes=32 * 1024 * 1024),
        cost_estimate=pl.CostEstimate(flops=weight, bytes_accessed=1, transcendentals=0),
    )


def band(halo, aligned, keys_in, values_in, queries_in, grad_in, lower, gain_rows):
    pair_count, rows, width = queries_in.shape
    score_scale = 1.0 / math.sqrt(width)
    factor = score_scale * LOG2E
    bf16, f32 = jnp.bfloat16, jnp.float32
    key_halo = shift(keys_in[:, rows - halo :], "ctx", 1)
    value_halo = shift(values_in[:, rows - halo :], "ctx", 1)

    row_spec = whole((rows, width))
    gain_spec = whole((1, width))
    stat_spec = whole((8, rows))
    delta_spec = whole((1, rows))
    halo_spec = whole((halo, width))
    ridden_spec = whole((halo + RIDERS, width))
    keyt_spec = whole((width, rows))
    own_sq = whole((rows, rows))
    halo_sq = whole((halo, rows))
    low_spec = pl.BlockSpec((1, rows), lambda p: (0, 0))

    def shaped(shape, dtype):
        return jax.ShapeDtypeStruct((pair_count,) + shape, dtype)

    row_out = (row_spec, shaped((rows, width), bf16))
    wide_out = (row_spec, shaped((rows, width), f32))
    scaled, key_cols, part, own_weights, own_slopes = call(
        own_stats_kernel,
        pair_count,
        [row_spec] * 4 + [gain_spec, low_spec],
        (
            row_out,
            (keyt_spec, shaped((width, rows), bf16)),
            (stat_spec, shaped((8, rows), f32)),
            (own_sq, shaped((rows, rows), f32)),
            (own_sq, shaped((rows, rows), f32)),
        ),
        LIGHT,
        factor=factor,
        step=BLK if halo >= LONG * BLK else GROUP,
    )(queries_in, keys_in, values_in, grad_in, gain_rows, lower)

    own_delta, halo_probs, own_probs, dv_halo = call(
        probs_kernel,
        pair_count,
        [row_spec, row_spec, low_spec, stat_spec, own_sq, halo_spec],
        (
            (delta_spec, shaped((1, rows), f32)),
            (halo_sq, shaped((halo, rows), bf16)),
            (own_sq, shaped((rows, rows), bf16)),
            (halo_spec, shaped((halo, width), bf16)),
        ),
        LIGHT,
        scratch=[pltpu.VMEM((1, rows), f32)],
        factor=factor,
        step=GROUP,
    )(scaled, grad_in, lower, part, own_weights, key_halo)
    dv_back = shift(dv_halo, "ctx", -1)

    dq, dk_halo, head_terms, own_grads = call(
        grads_kernel,
        pair_count,
        [row_spec] * 3 + [keyt_spec, delta_spec, halo_sq, own_sq, own_sq, halo_spec, halo_spec],
        (
            wide_out,
            (ridden_spec, shaped((halo + RIDERS, width), bf16)),
            (gain_spec, shaped((1, width), f32)),
            (own_sq, shaped((rows, rows), bf16)),
        ),
        HEAVY,
        scratch=[pltpu.VMEM((halo, rows), bf16)],
        score_scale=score_scale,
    )(
        queries_in, scaled, grad_in, key_cols, own_delta, halo_probs, own_probs, own_slopes,
        key_halo, value_halo,
    )
    dk_back = shift(dk_halo, "ctx", -1)
    length = lax.axis_size("ctx")
    riding = aligned and 1 < length <= 4
    terms = [head_terms]
    if riding:
        terms += [shift(head_terms, "ctx", by) for by in range(1, length - 1)]
    elif aligned:
        terms = [lax.psum(head_terms, "ctx")]

    grad_queries, grad_values, dk_own = call(
        own_keys_kernel,
        pair_count,
        [row_spec, row_spec, own_sq, own_sq, row_spec, gain_spec, halo_spec],
        (row_out, row_out, wide_out),
        10**9,
        scratch=[pltpu.VMEM((rows, width), f32)],
        score_scale=score_scale,
        step=BLK if halo >= LONG * BLK else GROUP,
    )(grad_in, scaled, own_probs, own_grads, dq, gain_rows, dv_back)
    grad_keys, gain_sum = call(
        finish_kernel,
        pair_count,
        [row_spec, ridden_spec] + [gain_spec] * len(terms),
        (row_out, (gain_spec, shaped((1, width), f32))),
        LIGHT,
        riding=riding,
    )(dk_own, dk_back, *terms)
    return grad_queries, grad_keys, grad_values, gain_sum


def on_device(queries, keys, values, grad_out, gain, doc_start, win_start):
    pair_count, rows, width = queries.shape
    head_first = lax.axis_index("dp") * pair_count % HEADS
    aligned = lax.axis_size("dp") * pair_count == HEADS and gain.shape[0] == pair_count * width
    if aligned:
        gain_rows = gain.reshape(pair_count, 1, width)
    else:
        full_gain = lax.all_gather(gain, "dp", axis=0, tiled=True)
        gain_rows = lax.dynamic_slice_in_dim(
            full_gain.reshape(HEADS, width), head_first, pair_count, 0
        ).reshape(pair_count, 1, width)

    hbm = pl.BlockSpec(memory_space=pltpu.HBM)
    row_out = (whole((rows, width)), jax.ShapeDtypeStruct((pair_count, rows, width), jnp.bfloat16))
    *loaded, size = call(
        load_kernel,
        pair_count,
        [hbm] * 6,
        [row_out] * 4
        + [
            (pl.BlockSpec((1, rows), lambda p: (0, 0)), jax.ShapeDtypeStruct((1, rows), jnp.int32)),
            (pl.BlockSpec(memory_space=pltpu.SMEM), jax.ShapeDtypeStruct((1,), jnp.int32)),
        ],
        LIGHT,
        scratch=[pltpu.VMEM(doc_start.shape, jnp.int32)] * 2 + [pltpu.SemaphoreType.DMA((6,))],
    )(*(pltpu.with_memory_space_constraint(x, pltpu.HBM) for x in (doc_start, win_start, keys, values, queries, grad_out)))
    grad_queries, grad_keys, grad_values, gain_sum = lax.switch(
        size[0],
        [functools.partial(band, blocks * BLK, aligned) for blocks in range(FEWEST, WBLK)],
        *loaded, gain_rows,
    )
    if aligned:
        grad_gain = gain_sum.reshape(pair_count * width)
    else:
        gain_table = lax.dynamic_update_slice_in_dim(
            jnp.zeros((HEADS, width), jnp.float32), gain_sum.reshape(pair_count, width), head_first, 0
        ).reshape(HEADS * width)
        everything = lax.psum(gain_table, ("ctx", "dp"))
        share = gain.shape[0]
        grad_gain = lax.dynamic_slice_in_dim(everything, lax.axis_index("dp") * share, share, 0)
    return (grad_queries, grad_keys, grad_values, grad_gain)


def solution(mesh):
    rows = P("dp", "ctx", None)
    return jax.shard_map(
        on_device,
        mesh=mesh,
        in_specs=(rows, rows, rows, rows, P("dp"), P(), P()),
        out_specs=(rows, rows, rows, P("dp")),
        check_vma=False,
    )
```
